32 devices in a mesh: ctx: 8 (over y, x, core), fsdp: 4 (over z).
Axes of the slice: x: 2, y: 2, z: 4, core: 2. Of those that a mesh axis runs over, the one named last changes fastest.
Arguments:
- query_in: bfloat16 [4, 1024, 2048], P('fsdp', 'ctx'), may hold values from -6 to 6
- key_in: bfloat16 [4, 1024, 2048], P('fsdp', 'ctx'), may hold values from -6 to 6
- value_in: bfloat16 [4, 1024, 2048], P('fsdp', 'ctx'), may hold values from -6 to 6
- feature_taps: float32 [3, 3, 2048], replicated, may hold values from -3 to 3
- decay_rate: float32 [128, 16], replicated, as said below
- residues: float32 [128, 16], replicated, may hold values from -3 to 3
- skip_gain: float32 [2048], replicated, may hold values from 0.5 to 1.5
- out_weight: bfloat16 [2048, 2048], P('fsdp'), may hold values from -0.1875 to 0.1875
Outputs:
- block_out: bfloat16 [4, 1024, 2048], P('fsdp', 'ctx')
The draws below stay inside these ranges and needn't reach their ends.
Inputs may be any that keep to these rules, and one draw needn't show every extreme that they name: `decay_rate`: every rate is positive.
All inputs are finite; a program needn't handle non-finite values.
Results may differ from the reference program's by a relative error of at most 0.0062.
Values may be sent and summed in bfloat16 or wider, within the bound.
No kernel may reach another device: no remote copies, remote signals or barrier semaphores. Data moves between devices by JAX's collectives and lax.ppermute only.
A program may use at most 128 MiB of HBM per device.

```python
import math
import jax
import jax.numpy as jnp
from jax import lax

C = 2048
DOUT = 2048
GROUP = 16
MODES = 16
FEAT = 3
GROUPS = 128
LEN = 1024
SEQS = 4


def draw_decay_rate(key, part):
    coin_key = jax.random.fold_in(key, 11)
    slow_key = jax.random.fold_in(key, 12)
    fast_key = jax.random.fold_in(key, 13)
    share = 0.5
    slow = jnp.exp(jax.random.uniform(slow_key, (GROUPS, MODES), jnp.float32, math.log(0.1), math.log(2.0))) / LEN
    fast = jnp.exp(jax.random.uniform(fast_key, (GROUPS, MODES), jnp.float32, math.log(1.0 / 50.0), math.log(1.0 / 30.0)))
    picked = jax.random.bernoulli(coin_key, share, (GROUPS, MODES))
    return jnp.where(picked, slow, fast).astype(jnp.float32)


def with_spikes(drawn, stream_key, source, target, parts, factor):
    def block_of(position):
        return (jnp.arange(drawn.shape[position]) // (drawn.shape[position] // parts)).reshape((-1,) + (1,) * (drawn.ndim - 1 - position))

    near = jax.random.permutation(stream_key, parts)[block_of(target)]
    far = (block_of(target) + parts // 2) % parts
    return jnp.where((block_of(source) == near) | (block_of(source) == far), factor * drawn, drawn)


def block_levels(own_key, shape, shards, smallest, largest):
    factor_of, own = 1.0, jax.random.fold_in(own_key, 6)
    for dim, shards_of in shards:
        steps = jnp.exp(jax.random.uniform(jax.random.fold_in(own, dim), (shards_of,), jnp.float32, smallest / len(shards), largest / len(shards)))
        factor_of = factor_of * jnp.repeat(steps, shape[dim] // shards_of).reshape([-1 if axis == dim else 1 for axis in range(len(shape))])
    return factor_of


def bell_draw(key, extent, width, most, cuts=(), dtype=jnp.bfloat16):
    array = jax.random.normal(key, extent, jnp.float32) * width
    if len(cuts) > 0:
        array = block_levels(key, extent, cuts, -0.22, 0.18) * array
    return jnp.clip(array, min=-most, max=most).astype(dtype)


def gaussian_with(rng, extent, deviation, reach, split, heavy, kind=jnp.bfloat16):
    array = deviation * jax.random.normal(rng, extent, jnp.float32)
    if split:
        array = array * block_levels(rng, extent, split, -0.22, 0.18)
    return jnp.clip(with_spikes(array, jax.random.fold_in(rng, 3), *heavy), -reach, reach).astype(kind)


def setup_inputs(seed: int = 0) -> dict:
    key_of = jax.random.split(jax.random.key(seed), 9)
    return {
        "query_in": bell_draw(key_of[0], (SEQS, LEN, C), 1.0, 6.0, ((0, 4), (1, 8))),
        "key_in": bell_draw(key_of[1], (SEQS, LEN, C), 1.0, 6.0, ((0, 4), (1, 8))),
        "value_in": bell_draw(key_of[2], (SEQS, LEN, C), 1.0, 6.0, ((0, 4), (1, 8))),
        "feature_taps": bell_draw(key_of[3], (3, FEAT, C), 0.5, 3.0, (), jnp.float32),
        "decay_rate": draw_decay_rate(jax.random.fold_in(key_of[8], 71), 0),
        "residues": bell_draw(key_of[5], (GROUPS, MODES), 0.5, 3.0, (), jnp.float32),
        "skip_gain": jnp.clip(jax.random.uniform(key_of[6], (C,), jnp.float32, 0.5, 1.5), 0.5, 1.5),
        "out_weight": gaussian_with(key_of[7], (C, DOUT), C ** -0.5, 0.1875, ((0, 4),), (0, 1, 4, 2.0)),
    }


def featurize(rows, taps_one):
    values = rows.astype(jnp.float32)
    total = taps_one[0] * values
    for offset in range(1, FEAT):
        moved = jnp.concatenate([jnp.zeros((offset, values.shape[1]), jnp.float32), values[:-offset]], axis=0)
        total = total + taps_one[offset] * moved
    return total

def group_filter(rate_row, residue_row, length):
    steps_axis = jnp.arange(length).astype(jnp.float32)
    scale = residue_row * jnp.sqrt(-jnp.expm1(-2.0 * rate_row))
    return lax.optimization_barrier(jnp.sum(scale[:, None] * jnp.exp(-rate_row[:, None] * steps_axis[None, :]), axis=0))

def group_conv(operands):
    rate_row, residue_row, signal = operands
    length = signal.shape[0]
    kernel = group_filter(rate_row, residue_row, length)
    spectrum = jnp.fft.rfft(kernel, 2 * length)
    signal_spec = jnp.fft.rfft(signal, 2 * length, axis=0)
    return jnp.fft.irfft(spectrum[:, None] * signal_spec, 2 * length, axis=0)[:length]

def one_sequence(query_rows, key_rows, value_rows, feature_taps, decay_rate, residues, skip_gain, out_weight):
    featured_q = featurize(query_rows, feature_taps[0])
    featured_k = featurize(key_rows, feature_taps[1])
    featured_v = featurize(value_rows, feature_taps[2])
    kv_round = lax.optimization_barrier((featured_k * featured_v).astype(jnp.bfloat16))
    kv_float = kv_round.astype(jnp.float32)
    length = kv_float.shape[0]
    grouped = jnp.transpose(kv_float.reshape(length, GROUPS, GROUP), (1, 0, 2))
    conv_groups = lax.map(group_conv, (decay_rate, residues, grouped))
    conv_rows = jnp.transpose(conv_groups, (1, 0, 2)).reshape(length, C)
    convolved = lax.optimization_barrier(conv_rows.astype(jnp.bfloat16))
    gated = (featured_q * (convolved.astype(jnp.float32) + skip_gain * kv_float)).astype(jnp.bfloat16)
    return jnp.dot(gated, out_weight, preferred_element_type=jnp.float32).astype(jnp.bfloat16)

def reference(query_in, key_in, value_in, feature_taps, decay_rate, residues, skip_gain, out_weight):
    results = []
    for number in range(SEQS):
        results.append(one_sequence(query_in[number], key_in[number], value_in[number], feature_taps, decay_rate, residues, skip_gain, out_weight))
    return jnp.stack(results)
```

```python
import functools

import jax
import jax.numpy as jnp
from jax import lax
from jax.experimental import pallas as pl
from jax.experimental.pallas import tpu as pltpu
from jax.sharding import PartitionSpec as P

GROUP = 16
FEAT = 3
WIDE = 256
VMEM_LIMIT = 48 << 20

bf16 = jnp.bfloat16
f32 = jnp.float32


def after(x, *deps):
    return lax.optimization_barrier((x,) + deps)[0]


def params():
    return pltpu.CompilerParams(vmem_limit_bytes=VMEM_LIMIT)


def split(x):
    high = x.astype(bf16)
    return high, (x - high.astype(f32)).astype(bf16)


def iota(shape, dim):
    return lax.broadcasted_iota(jnp.int32, shape, dim)


def dot(a, b):
    return jnp.dot(a, b, preferred_element_type=f32)


def featurize(rows, tail, taps):
    values = rows.astype(f32)
    at = iota(values.shape, 0)
    one = jnp.where(at == 0, tail[1:2], pltpu.roll(values, 1, 0))
    two = jnp.where(at == 0, tail[0:1], jnp.where(at == 1, tail[1:2], pltpu.roll(values, 2, 0)))
    return taps[0:1] * values + taps[1:2] * one + taps[2:3] * two


def closing_kernel(rate_ref, scale_ref, out_ref):
    rows = out_ref.shape[1] // 2
    back = (rows - 1 - iota((rows, WIDE), 0)).astype(f32)
    table = jnp.exp(-rate_ref[0] * back) * scale_ref[0]
    high, low = split(table.T)
    out_ref[:, :rows] = high
    out_ref[:, rows:] = low


def product_kernel(key_ref, value_ref, halo_ref, taps_ref, closing_ref, kv_ref, state_ref):
    halo = halo_ref[...]
    key = featurize(key_ref[...], halo[2:4], taps_ref[1])
    value = featurize(value_ref[...], halo[4:6], taps_ref[2])
    kv = (key * value).astype(bf16)
    kv_ref[...] = kv
    ends = dot(closing_ref[...], jnp.concatenate([kv, kv], axis=0))
    modes = state_ref.shape[0]
    owner = iota((modes, WIDE), 1) // GROUP
    total = jnp.zeros((modes, WIDE), f32)
    for g in range(WIDE // GROUP):
        total = jnp.where(owner == g, ends[g * modes : (g + 1) * modes], total)
    state_ref[...] = total


def inner_kernel(rate_ref, scale_ref, kv_ref, out_ref):
    rows = kv_ref.shape[0]
    groups, modes = rate_ref.shape
    at = iota((groups, rows), 1)
    lag = jnp.where(at == 0, 0, rows - at).astype(f32)
    taps = jnp.zeros((groups, rows), f32)
    for n in range(modes):
        taps = taps + scale_ref[:, n : n + 1] * jnp.exp(-rate_ref[:, n : n + 1] * lag)
    kv = kv_ref[...]
    twice = jnp.concatenate([kv, kv], axis=0)
    causal = iota((rows, rows), 0) >= iota((rows, rows), 1)
    owner = iota((rows, WIDE), 1) // GROUP
    total = jnp.zeros((rows, WIDE), f32)
    for g in range(groups):
        band = jnp.broadcast_to(taps[g : g + 1], (rows, rows))
        band = pltpu.roll(band, 0, 1, stride=1, stride_axis=0)
        high, low = split(jnp.where(causal, band, 0.0))
        part = dot(jnp.concatenate([high, low], axis=1), twice)
        total = jnp.where(owner == g, part, total)
    out_ref[...] = total


def gate_kernel(query_ref, halo_ref, taps_ref, kv_ref, inner_ref, enter_ref, rate_ref, skip_ref, out_ref):
    rows = query_ref.shape[0]
    query = featurize(query_ref[...], halo_ref[0:2], taps_ref[0])
    ahead = (iota((rows, WIDE), 0) + 1).astype(f32)
    lag_high, lag_low = split(jnp.exp(-rate_ref[0] * ahead))
    enter = enter_ref[...]
    modes = enter.shape[0]
    spread = jnp.concatenate([enter] * (WIDE // modes), axis=0)
    same = iota((WIDE, WIDE), 0) // modes == iota((WIDE, WIDE), 1) // GROUP
    in_high, in_low = split(jnp.where(same, spread, 0.0))
    cross = dot(lag_high, in_high) + dot(lag_low, in_high) + dot(lag_high, in_low)
    convolved = (inner_ref[...] + cross).astype(bf16).astype(f32)
    kv = kv_ref[...].astype(f32)
    out_ref[...] = (query * (convolved + skip_ref[...] * kv)).astype(bf16)


def wide(rows):
    return pl.BlockSpec((rows, WIDE), lambda b: (0, b))


def conv_path(query, key, value, taps, rate, residues, skip):
    rows, chans = query.shape
    modes = rate.shape[1]
    blocks = chans // WIDE
    count = lax.axis_size("ctx")
    index = lax.axis_index("ctx")
    scale = residues * jnp.sqrt(-jnp.expm1(-2.0 * rate))
    rate_row = rate.reshape(blocks, 1, WIDE)
    scale_row = scale.reshape(blocks, 1, WIDE)
    keep = FEAT - 1
    tails = jnp.concatenate(
        [query[rows - keep :], key[rows - keep :], value[rows - keep :], query[rows - keep :]]
    ).astype(f32)
    halo = lax.ppermute(tails, "ctx", [(i, i + 1) for i in range(count - 1)])
    row_spec = pl.BlockSpec((1, 1, WIDE), lambda b: (b, 0, 0))
    taps_spec = pl.BlockSpec((3, FEAT, WIDE), lambda b: (0, 0, b))
    mode_spec = pl.BlockSpec((WIDE // GROUP, modes), lambda b: (b, 0))
    closing = pl.pallas_call(
        closing_kernel,
        grid=(blocks,),
        in_specs=[row_spec, row_spec],
        out_specs=pl.BlockSpec((WIDE, 2 * rows), lambda b: (b, 0)),
        out_shape=jax.ShapeDtypeStruct((blocks * WIDE, 2 * rows), bf16),
        compiler_params=params(),
        name="closing_table",
    )(rate_row, scale_row)
    kv, state = pl.pallas_call(
        product_kernel,
        grid=(blocks,),
        in_specs=[
            wide(rows),
            wide(rows),
            wide(8),
            taps_spec,
            pl.BlockSpec((WIDE, 2 * rows), lambda b: (b, 0)),
        ],
        out_specs=[wide(rows), wide(modes)],
        out_shape=[
            jax.ShapeDtypeStruct((rows, chans), bf16),
            jax.ShapeDtypeStruct((modes, chans), f32),
        ],
        compiler_params=params(),
        name="kv_and_state",
    )(key, value, halo, taps, closing)
    inner = pl.pallas_call(
        inner_kernel,
        grid=(blocks,),
        in_specs=[mode_spec, mode_spec, wide(rows)],
        out_specs=wide(rows),
        out_shape=jax.ShapeDtypeStruct((rows, chans), f32),
        compiler_params=params(),
        name="inner_conv",
    )(rate, scale, kv)
    rate_chan = jnp.repeat(rate.T, GROUP, axis=1)
    enter = jnp.zeros_like(state)
    step = 1
    while step < count:
        other = lax.ppermute(state, "ctx", [(i, i ^ step) for i in range(count)])
        upper = (index // step) % 2 == 1
        within = (index % step * rows).astype(f32)
        enter = jnp.where(upper, enter + jnp.exp(-rate_chan * within) * other, enter)
        fade = jnp.exp(-rate_chan * float(step * rows))
        state = jnp.where(upper, other * fade + state, state * fade + other)
        step *= 2
    return pl.pallas_call(
        gate_kernel,
        grid=(blocks,),
        in_specs=[
            wide(rows),
            wide(8),
            taps_spec,
            wide(rows),
            wide(rows),
            wide(modes),
            row_spec,
            wide(1),
        ],
        out_specs=wide(rows),
        out_shape=jax.ShapeDtypeStruct((rows, chans), bf16),
        compiler_params=params(),
        name="gate",
    )(query, halo, taps, kv, inner, enter, rate_row, skip[None])


def hop(x, first):
    count = lax.axis_size("ctx")
    even, odd = (2, 4) if first else (4, 2)
    return lax.ppermute(x, "ctx", [(i, i ^ (odd if i % 2 else even)) for i in range(count)])


def gather_weight(weight):
    index = lax.axis_index("ctx")
    place = lax.axis_index("fsdp")
    depth, cols = weight.shape
    block = cols // 8
    inward = [(1, 2), (2, 1)]
    outward = [(1, 0), (2, 3)]
    middle = (place == 1) | (place == 2)
    mine = lax.dynamic_slice(weight, (0, (index % 8) * block), (depth, block))
    near = lax.ppermute(mine, "fsdp", [(i, i ^ 1) for i in range(4)])
    across = lax.ppermute(mine, "fsdp", inward)
    far = lax.ppermute(mine, "fsdp", [(0, 2), (3, 1)])
    slots = []
    one_a, one_b = hop(near, True), hop(near, False)
    out_two = lax.ppermute(across, "fsdp", outward)
    one_c = hop(one_a, False)
    slots.append((near, one_a, one_b, one_c))
    two = jnp.where(middle, across, after(out_two, one_a))
    two_a, two_b = hop(two, True), hop(two, False)
    out_three = lax.ppermute(after(far, out_two), "fsdp", outward)
    two_c = hop(two_a, False)
    slots.append((two, two_a, two_b, two_c))
    three = jnp.where(middle, far, after(out_three, two_a, one_c))
    three_a, three_b = hop(three, True), hop(three, False)
    three_c = hop(after(three_a, two_c, two_b), False)
    slots.append((three, three_a, three_b, three_c))
    return slots


def matmul_kernel(slot_count, has_own, has_acc, last, nums_ref, *refs):
    refs = list(refs)
    mine_ref, other_ref = refs[0], refs[1]
    refs = refs[2:]
    if has_own:
        weight_ref = refs.pop(0)
    slots = [refs[4 * s : 4 * s + 4] for s in range(slot_count)]
    refs = refs[4 * slot_count :]
    if has_acc:
        acc_ref = refs.pop(0)
    rows = mine_ref.shape[0]
    depth, block = slots[0][0].shape

    def rows_of(part):
        at = pl.multiple_of(nums_ref[part] * depth, depth)
        return jnp.concatenate(
            [mine_ref[:, pl.ds(at, depth)], other_ref[:, pl.ds(at, depth)]], axis=0
        )

    lhs = [rows_of(1 + s) for s in range(slot_count)]
    if has_own:
        own = rows_of(0)
    for r in range(4):
        total = acc_ref[:, r * block : (r + 1) * block] if has_acc else None
        if has_own:
            at = pl.multiple_of(nums_ref[4 + r] * block, block)
            total = dot(own, weight_ref[:, pl.ds(at, block)])
        for s in range(slot_count):
            part = dot(lhs[s], slots[s][r][...])
            total = part if total is None else total + part
        if last:
            at = pl.multiple_of(nums_ref[8 + r] * block, block)
            done = total.astype(bf16)
            refs[0][:, pl.ds(at, block)] = done[:rows]
            refs[1][:, pl.ds(at, block)] = done[rows:]
        else:
            refs[0][:, r * block : (r + 1) * block] = total


def join_kernel(nums_ref, mine_ref, other_ref, out_ref):
    block = mine_ref.shape[1] // 4
    core = nums_ref[0]
    for h in range(4):
        at = pl.multiple_of((2 * h + core) * block, block)
        out_ref[:, pl.ds(at, block)] = mine_ref[:, h * block : (h + 1) * block]
        at = pl.multiple_of((2 * h + 1 - core) * block, block)
        out_ref[:, pl.ds(at, block)] = other_ref[:, h * block : (h + 1) * block]


def project(gated, weight, slots):
    count = lax.axis_size("ctx")
    index = lax.axis_index("ctx")
    place = lax.axis_index("fsdp")
    rows = gated.shape[0]
    depth, cols = weight.shape
    half = cols // 2
    swap = [(i, i ^ 1) for i in range(count)]
    other = lax.ppermute(gated, "ctx", swap)
    core = index % 2
    first, second = jnp.where(core == 0, 2, 4), jnp.where(core == 0, 4, 2)
    rel = index % 8
    order = [rel, rel ^ first, rel ^ second, rel ^ 6]
    parts = [
        place,
        place ^ 1,
        jnp.where(place <= 1, 2, 1),
        jnp.where(place <= 1, 3, 0),
    ]
    nums = jnp.stack(parts + order + [n // 2 for n in order]).astype(jnp.int32)
    vmem = pl.BlockSpec(memory_space=pltpu.VMEM)
    smem = pl.BlockSpec(memory_space=pltpu.SMEM)
    acc = pl.pallas_call(
        functools.partial(matmul_kernel, 2, True, False, False),
        in_specs=[smem] + [vmem] * 11,
        out_specs=vmem,
        out_shape=jax.ShapeDtypeStruct((2 * rows, half), f32),
        compiler_params=params(),
        name="project_near",
    )(nums, gated, other, weight, *slots[0], *slots[1])
    late = nums.at[1].set(nums[3])
    mine, theirs = pl.pallas_call(
        functools.partial(matmul_kernel, 1, False, True, True),
        in_specs=[smem] + [vmem] * 7,
        out_specs=[vmem, vmem],
        out_shape=[jax.ShapeDtypeStruct((rows, half), bf16)] * 2,
        compiler_params=params(),
        name="project_far",
    )(late, gated, other, *slots[2], acc)
    back = lax.ppermute(theirs, "ctx", swap)
    return pl.pallas_call(
        join_kernel,
        in_specs=[smem, vmem, vmem],
        out_specs=vmem,
        out_shape=jax.ShapeDtypeStruct((rows, cols), bf16),
        compiler_params=params(),
        name="join_columns",
    )(core[None].astype(jnp.int32), mine, back)


def local(query_in, key_in, value_in, feature_taps, decay_rate, residues, skip_gain, out_weight):
    gated = conv_path(
        query_in[0], key_in[0], value_in[0], feature_taps, decay_rate, residues, skip_gain
    )
    return project(gated, out_weight, gather_weight(out_weight))[None]


def solution(mesh):
    return jax.shard_map(
        local,
        mesh=mesh,
        in_specs=(
            P("fsdp", "ctx", None),
            P("fsdp", "ctx", None),
            P("fsdp", "ctx", None),
            P(),
            P(),
            P(),
            P(),
            P("fsdp", None),
        ),
        out_specs=P("fsdp", "ctx", None),
        check_vma=False,
    )
```

```python
import functools

import jax
import jax.numpy as jnp
from jax import lax
from jax.experimental import pallas as pl
from jax.experimental.pallas import tpu as pltpu
from jax.sharding import PartitionSpec as P

GROUP = 16
FEAT = 3
WIDE = 512
LANES = 128
SUB = 32
VMEM_LIMIT = 48 << 20

bf16 = jnp.bfloat16
f32 = jnp.float32


def after(x, *deps):
    return lax.optimization_barrier((x,) + deps)[0]


def params():
    return pltpu.CompilerParams(vmem_limit_bytes=VMEM_LIMIT)


def split(x):
    high = x.astype(bf16)
    return high, (x - high.astype(f32)).astype(bf16)


def iota(shape, dim):
    return lax.broadcasted_iota(jnp.int32, shape, dim)


def one_less_exp(x):
    small = jnp.minimum(x, 0.5)
    series = jnp.ones_like(x)
    for n in range(9, 1, -1):
        series = 1.0 - small * (1.0 / n) * series
    return jnp.where(x < 0.5, small * series, 1.0 - jnp.exp(-x))


def dot(a, b):
    return jnp.dot(a, b, preferred_element_type=f32)


def featurize(rows, tail, taps):
    values = rows.astype(f32)
    at = iota(values.shape, 0)
    one = jnp.where(at == 0, tail[1:2], pltpu.roll(values, 1, 0))
    two = jnp.where(at == 0, tail[0:1], jnp.where(at == 1, tail[1:2], pltpu.roll(values, 2, 0)))
    return taps[0:1] * values + taps[1:2] * one + taps[2:3] * two


def table_kernel(rate_ref, residue_ref, left_ref, lag_ref, rate_chan_ref):
    rate = rate_ref[...]
    groups, modes = rate.shape
    scale = residue_ref[...] * jnp.sqrt(one_less_exp(2.0 * rate))
    blocks, _, depth = left_ref.shape
    sub = left_ref.shape[1] // 2 - modes
    each = groups // blocks

    def expand(table, width, count, first):
        pick = iota((groups, count), 0) == first + iota((groups, count), 1) // width
        return lax.dot_general(
            table,
            pick.astype(f32),
            (((0,), (0,)), ((), ())),
            precision=lax.Precision.HIGHEST,
            preferred_element_type=f32,
        )

    rate_chan_ref[...] = expand(rate, GROUP, groups * GROUP, 0)
    rate_wide = expand(rate, sub, groups * sub, 0)
    scale_wide = expand(scale, sub, groups * sub, 0)
    place = iota((modes, groups * sub), 1) % sub
    back = jnp.where(place == 0, 0, sub - place).astype(f32)
    taps = jnp.sum(scale_wide * jnp.exp(-rate_wide * back), axis=0, keepdims=True)
    ends = scale_wide * jnp.exp(-rate_wide * (sub - 1 - place).astype(f32))
    end_high, end_low = split(ends)
    causal = iota((sub, LANES), 0) >= iota((sub, LANES), 1) % sub
    start = iota((1, LANES), 1) % sub == 0
    mode_pick = iota((modes, each * modes), 0) == iota((modes, each * modes), 1) % modes
    group_at = iota((groups, each * modes), 1) // modes
    ahead = (iota((sub, each * modes), 0) + 1).astype(f32)
    for b in range(blocks):
        for part in range(depth // LANES):
            at = b * depth + part * LANES
            row = taps[:, at : at + LANES]
            row = jnp.where(start, row, pltpu.roll(row, LANES - sub, 1))
            band = pltpu.roll(jnp.broadcast_to(row, (sub, LANES)), 0, 1, stride=1, stride_axis=0)
            high, low = split(jnp.where(causal, band, 0.0))
            to = slice(part * LANES, (part + 1) * LANES)
            left_ref[b, :sub, to] = high
            left_ref[b, sub : 2 * sub, to] = low
        cols = slice(b * depth, (b + 1) * depth)
        left_ref[b, 2 * sub : 2 * sub + modes] = end_high[:, cols]
        left_ref[b, 2 * sub + modes :] = end_low[:, cols]
        spread = jnp.dot(
            (iota((groups, each * modes), 0) == b * each + group_at).astype(f32).T,
            rate,
            precision=lax.Precision.HIGHEST,
            preferred_element_type=f32,
        )
        rate_lane = jnp.sum(jnp.where(mode_pick, spread.T, 0.0), axis=0, keepdims=True)
        high, low = split(jnp.exp(-rate_lane * ahead))
        lag_ref[b, :sub] = jnp.concatenate([high, high], axis=1)
        lag_ref[b, sub:] = jnp.concatenate([low, jnp.zeros_like(low)], axis=1)


def own_groups(rows_each):
    rows = LANES // GROUP * rows_each
    return iota((rows, LANES), 0) // rows_each == iota((rows, LANES), 1) // GROUP


def product_kernel(
    key_ref, value_ref, halo_ref, taps_ref, left_ref, rate_ref, kv_ref, inner_ref, before_ref, state_ref
):
    rows, width = key_ref.shape
    modes = rate_ref.shape[0]
    sub = left_ref.shape[1] // 2 - modes
    count = rows // sub
    halo = halo_ref[...]
    key = featurize(key_ref[...], halo[2:4], taps_ref[1])
    value = featurize(value_ref[...], halo[4:6], taps_ref[2])
    kv = (key * value).astype(bf16)
    kv_ref[...] = kv
    same = own_groups(sub)
    fade = jnp.exp(-rate_ref[...] * float(sub))
    for b in range(width // LANES):
        cols = slice(b * LANES, (b + 1) * LANES)
        total = jnp.zeros((modes, LANES), f32)
        for first in range(0, count, 2):
            right = []
            for s in (first, first + 1):
                piece = kv[s * sub : (s + 1) * sub, cols]
                spread = jnp.concatenate([piece] * (LANES // GROUP), axis=0)
                right.append(jnp.where(same, spread, jnp.zeros_like(spread)))
            out = dot(left_ref[b], jnp.concatenate(right, axis=1))
            for s in (first, first + 1):
                part = out[:, (s - first) * LANES : (s - first + 1) * LANES]
                inner_ref[s * sub : (s + 1) * sub, cols] = part[:sub] + part[sub : 2 * sub]
                before_ref[s * modes : (s + 1) * modes, cols] = total
                total = total * fade[:, cols] + (
                    part[2 * sub : 2 * sub + modes] + part[2 * sub + modes :]
                )
        state_ref[:, cols] = total


def blend_kernel(rows, step, where_ref, state_ref, other_ref, enter_ref, rate_ref, new_ref, into_ref):
    index = where_ref[0]
    upper = (index // step) % 2 == 1
    within = ((index % step) * rows).astype(f32)
    rate = rate_ref[...]
    state, other, enter = state_ref[...], other_ref[...], enter_ref[...]
    into_ref[...] = jnp.where(upper, enter + jnp.exp(-rate * within) * other, enter)
    fade = jnp.exp(-rate * float(step * rows))
    new_ref[...] = jnp.where(upper, other * fade + state, state * fade + other)


def gate_kernel(
    step, where_ref, query_ref, halo_ref, taps_ref, kv_ref, inner_ref, before_ref, enter_ref, other_ref,
    rate_ref, lag_ref, skip_ref, out_ref,
):
    rows, width = query_ref.shape
    modes = rate_ref.shape[0]
    sub = lag_ref.shape[1] // 2
    index = where_ref[0]
    upper = (index // step) % 2 == 1
    within = ((index % step) * rows).astype(f32)
    query = featurize(query_ref[...], halo_ref[0:2], taps_ref[0])
    rate = rate_ref[...]
    enter = enter_ref[...]
    enter = jnp.where(upper, enter + jnp.exp(-rate * within) * other_ref[...], enter)
    fade = jnp.exp(-rate * float(sub))
    same = own_groups(modes)
    for b in range(width // LANES):
        cols = slice(b * LANES, (b + 1) * LANES)
        far = enter[:, cols]
        for first in range(0, rows // sub, 2):
            right = []
            for s in (first, first + 1):
                total = far + before_ref[s * modes : (s + 1) * modes, cols]
                spread = jnp.concatenate([total] * (LANES // GROUP), axis=0)
                right.append(jnp.concatenate(split(jnp.where(same, spread, 0.0)), axis=0))
                far = far * fade[:, cols]
            cross = dot(lag_ref[b], jnp.concatenate(right, axis=1))
            for s in (first, first + 1):
                part = cross[:, (s - first) * LANES : (s - first + 1) * LANES]
                at = slice(s * sub, (s + 1) * sub)
                convolved = inner_ref[at, cols] + (part[:sub] + part[sub:])
                convolved = convolved.astype(bf16).astype(f32)
                kv = kv_ref[at, cols].astype(f32)
                out_ref[at, cols] = (query[at, cols] * (convolved + skip_ref[:, cols] * kv)).astype(bf16)


def tail_kernel(query_ref, key_ref, value_ref, out_ref):
    keep = FEAT - 1
    for i, ref in enumerate((query_ref, key_ref, value_ref)):
        rows = ref[...].astype(f32)
        out_ref[i * keep : (i + 1) * keep] = rows[rows.shape[0] - keep :]
    out_ref[3 * keep :] = jnp.zeros((out_ref.shape[0] - 3 * keep, out_ref.shape[1]), f32)


def send_tails(query, key, value):
    rows, chans = query.shape
    count = lax.axis_size("ctx")
    last = pl.BlockSpec((16, chans), lambda i: (rows // 16 - 1, 0))
    tails = pl.pallas_call(
        tail_kernel,
        grid=(1,),
        in_specs=[last] * 3,
        out_specs=pl.BlockSpec((8, chans), lambda i: (0, 0)),
        out_shape=jax.ShapeDtypeStruct((8, chans), f32),
        compiler_params=params(),
        name="last_rows",
    )(query, key, value)
    return lax.ppermute(tails, "ctx", [(i, i + 1) for i in range(count - 1)])


def conv_path(query, key, value, halo, taps, rate, residues, skip):
    rows, chans = query.shape
    groups, modes = rate.shape
    count = lax.axis_size("ctx")
    here = lax.axis_index("ctx")[None].astype(jnp.int32)
    blocks = chans // LANES
    depth = LANES // GROUP * SUB
    steps = chans // WIDE
    per = WIDE // LANES
    vmem = pl.BlockSpec(memory_space=pltpu.VMEM)
    smem = pl.BlockSpec(memory_space=pltpu.SMEM)
    state_shape = jax.ShapeDtypeStruct((modes, chans), f32)
    left, lag, rate_chan = pl.pallas_call(
        table_kernel,
        in_specs=[vmem, vmem],
        out_specs=[vmem] * 3,
        out_shape=[
            jax.ShapeDtypeStruct((blocks, 2 * (SUB + modes), depth), bf16),
            jax.ShapeDtypeStruct((blocks, 2 * SUB, 2 * (LANES // GROUP) * modes), bf16),
            state_shape,
        ],
        compiler_params=params(),
        name="tables",
    )(rate, residues)

    def wide(height):
        return pl.BlockSpec((height, WIDE), lambda b: (0, b))

    def stack(array):
        return pl.BlockSpec((per,) + array.shape[1:], lambda b: (b, 0, 0))

    taps_spec = pl.BlockSpec((3, FEAT, WIDE), lambda b: (0, 0, b))
    subs = rows // SUB
    kv, inner, before, state = pl.pallas_call(
        product_kernel,
        grid=(steps,),
        in_specs=[wide(rows), wide(rows), wide(8), taps_spec, stack(left), wide(modes)],
        out_specs=[wide(rows), wide(rows), wide(subs * modes), wide(modes)],
        out_shape=[
            jax.ShapeDtypeStruct((rows, chans), bf16),
            jax.ShapeDtypeStruct((rows, chans), f32),
            jax.ShapeDtypeStruct((subs * modes, chans), f32),
            state_shape,
        ],
        compiler_params=params(),
        name="kv_and_state",
    )(key, value, halo, taps, left, rate_chan)
    enter = jnp.zeros_like(state)
    step = 1
    while True:
        other = lax.ppermute(state, "ctx", [(i, i ^ step) for i in range(count)])
        if 2 * step >= count:
            break
        state, enter = pl.pallas_call(
            functools.partial(blend_kernel, rows, step),
            in_specs=[smem] + [vmem] * 4,
            out_specs=[vmem] * 2,
            out_shape=[state_shape] * 2,
            compiler_params=params(),
            name="blend_states",
        )(here, state, other, enter, rate_chan)
        step *= 2
    return pl.pallas_call(
        functools.partial(gate_kernel, step),
        grid=(steps,),
        in_specs=[
            smem,
            wide(rows),
            wide(8),
            taps_spec,
            wide(rows),
            wide(rows),
            wide(subs * modes),
            wide(modes),
            wide(modes),
            wide(modes),
            stack(lag),
            wide(1),
        ],
        out_specs=wide(rows),
        out_shape=jax.ShapeDtypeStruct((rows, chans), bf16),
        compiler_params=params(),
        name="gate",
    )(here, query, halo, taps, kv, inner, before, enter, other, rate_chan, lag, skip[None])


def hop(x, first):
    count = lax.axis_size("ctx")
    even, odd = (2, 4) if first else (4, 2)
    return lax.ppermute(x, "ctx", [(i, i ^ (odd if i % 2 else even)) for i in range(count)])


def spread_slot(piece, *first):
    one, two = hop(piece, True), hop(piece, False)
    return piece, one, two, hop(after(one, *first), False)


def send_weight(weight):
    index = lax.axis_index("ctx")
    depth, cols = weight.shape
    block = cols // 8
    mine = lax.dynamic_slice(weight, (0, (index % 8) * block), (depth, block))
    near = lax.ppermute(mine, "fsdp", [(i, i ^ 1) for i in range(4)])
    return mine, near


def gather_weight(mine, near):
    two = lax.ppermute(mine, "fsdp", [(i, i ^ 2) for i in range(4)])
    three = lax.ppermute(mine, "fsdp", [(i, i ^ 3) for i in range(4)])
    slot_one = spread_slot(near)
    slot_two = spread_slot(after(two, slot_one[1]))
    slot_three = spread_slot(after(three, slot_two[1], *slot_one), *slot_two)
    return slot_one, slot_two, slot_three


def matmul_kernel(slot_count, has_own, has_acc, last, nums_ref, *refs):
    refs = list(refs)
    mine_ref, other_ref = refs[0], refs[1]
    refs = refs[2:]
    if has_own:
        weight_ref = refs.pop(0)
    slots = [refs[4 * s : 4 * s + 4] for s in range(slot_count)]
    refs = refs[4 * slot_count :]
    if has_acc:
        acc_ref = refs.pop(0)
    rows = mine_ref.shape[0]
    depth, block = slots[0][0].shape

    def rows_of(part):
        at = pl.multiple_of(nums_ref[part] * depth, depth)
        return jnp.concatenate(
            [mine_ref[:, pl.ds(at, depth)], other_ref[:, pl.ds(at, depth)]], axis=0
        )

    lhs = [rows_of(1 + s) for s in range(slot_count)]
    if has_own:
        own = rows_of(0)
    for r in range(4):
        total = acc_ref[:, r * block : (r + 1) * block] if has_acc else None
        if has_own:
            at = pl.multiple_of(nums_ref[4 + r] * block, block)
            total = dot(own, weight_ref[:, pl.ds(at, block)])
        for s in range(slot_count):
            part = dot(lhs[s], slots[s][r][...])
            total = part if total is None else total + part
        if last:
            at = pl.multiple_of(nums_ref[8 + r] * block, block)
            done = total.astype(bf16)
            refs[0][:, pl.ds(at, block)] = done[:rows]
            refs[1][:, pl.ds(at, block)] = done[rows:]
        else:
            refs[0][:, r * block : (r + 1) * block] = total


def join_kernel(nums_ref, mine_ref, other_ref, out_ref):
    block = mine_ref.shape[1] // 4
    core = nums_ref[0]
    for h in range(4):
        at = pl.multiple_of((2 * h + core) * block, block)
        out_ref[:, pl.ds(at, block)] = mine_ref[:, h * block : (h + 1) * block]
        at = pl.multiple_of((2 * h + 1 - core) * block, block)
        out_ref[:, pl.ds(at, block)] = other_ref[:, h * block : (h + 1) * block]


def project(gated, weight, slots):
    count = lax.axis_size("ctx")
    index = lax.axis_index("ctx")
    place = lax.axis_index("fsdp")
    rows = gated.shape[0]
    depth, cols = weight.shape
    half = cols // 2
    swap = [(i, i ^ 1) for i in range(count)]
    other = lax.ppermute(gated, "ctx", swap)
    core = index % 2
    first, second = jnp.where(core == 0, 2, 4), jnp.where(core == 0, 4, 2)
    rel = index % 8
    order = [rel, rel ^ first, rel ^ second, rel ^ 6]
    parts = [place, place ^ 1, place ^ 2, place ^ 3]
    nums = jnp.stack(parts + order + [n // 2 for n in order]).astype(jnp.int32)
    vmem = pl.BlockSpec(memory_space=pltpu.VMEM)
    smem = pl.BlockSpec(memory_space=pltpu.SMEM)
    acc = pl.pallas_call(
        functools.partial(matmul_kernel, 2, True, False, False),
        in_specs=[smem] + [vmem] * 11,
        out_specs=vmem,
        out_shape=jax.ShapeDtypeStruct((2 * rows, half), f32),
        compiler_params=params(),
        name="project_near",
    )(nums, gated, other, weight, *slots[0], *slots[1])
    late = nums.at[1].set(nums[3])
    mine, theirs = pl.pallas_call(
        functools.partial(matmul_kernel, 1, False, True, True),
        in_specs=[smem] + [vmem] * 7,
        out_specs=[vmem, vmem],
        out_shape=[jax.ShapeDtypeStruct((rows, half), bf16)] * 2,
        compiler_params=params(),
        name="project_far",
    )(late, gated, other, *slots[2], acc)
    back = lax.ppermute(theirs, "ctx", swap)
    return pl.pallas_call(
        join_kernel,
        in_specs=[smem, vmem, vmem],
        out_specs=vmem,
        out_shape=jax.ShapeDtypeStruct((rows, cols), bf16),
        compiler_params=params(),
        name="join_columns",
    )(core[None].astype(jnp.int32), mine, back)


def local(query_in, key_in, value_in, feature_taps, decay_rate, residues, skip_gain, out_weight):
    query, key, value = query_in[0], key_in[0], value_in[0]
    mine, near = send_weight(out_weight)
    halo = send_tails(query, key, value)
    gated = conv_path(query, key, value, halo, feature_taps, decay_rate, residues, skip_gain)
    return project(gated, out_weight, gather_weight(mine, near))[None]


def solution(mesh):
    return jax.shard_map(
        local,
        mesh=mesh,
        in_specs=(
            P("fsdp", "ctx", None),
            P("fsdp", "ctx", None),
            P("fsdp", "ctx", None),
            P(),
            P(),
            P(),
            P(),
            P("fsdp", None),
        ),
        out_specs=P("fsdp", "ctx", None),
        check_vma=False,
    )
```

```python
import functools

import jax
import jax.numpy as jnp
from jax import lax
from jax.experimental import pallas as pl
from jax.experimental.pallas import tpu as pltpu
from jax.sharding import PartitionSpec as P

GROUP = 16
FEAT = 3
WIDE = 512
LANES = 128
SUB = 32
VMEM_LIMIT = 48 << 20

bf16 = jnp.bfloat16
f32 = jnp.float32


def after(x, *deps):
    return lax.optimization_barrier((x,) + deps)[0]


def params(limit=VMEM_LIMIT):
    return pltpu.CompilerParams(vmem_limit_bytes=limit)


def split(x):
    high = x.astype(bf16)
    return high, (x - high.astype(f32)).astype(bf16)


def iota(shape, dim):
    return lax.broadcasted_iota(jnp.int32, shape, dim)


def one_less_exp(x):
    small = jnp.minimum(x, 0.5)
    series = jnp.ones_like(x)
    for n in range(9, 1, -1):
        series = 1.0 - small * (1.0 / n) * series
    return jnp.where(x < 0.5, small * series, 1.0 - jnp.exp(-x))


def dot(a, b):
    return jnp.dot(a, b, preferred_element_type=f32)


def featurize(rows, tail, taps):
    values = rows.astype(f32)
    at = iota(values.shape, 0)
    one = jnp.where(at == 0, tail[1:2], pltpu.roll(values, 1, 0))
    two = jnp.where(at == 0, tail[0:1], jnp.where(at == 1, tail[1:2], pltpu.roll(values, 2, 0)))
    return taps[0:1] * values + taps[1:2] * one + taps[2:3] * two


def table_kernel(rate_ref, residue_ref, left_ref, lag_ref, rate_chan_ref):
    rate = rate_ref[...]
    groups, modes = rate.shape
    scale = residue_ref[...] * jnp.sqrt(one_less_exp(2.0 * rate))
    blocks, _, depth = left_ref.shape
    sub = left_ref.shape[1] // 2 - modes
    each = groups // blocks

    def expand(table, width, count):
        pick = iota((groups, count), 0) == iota((groups, count), 1) // width
        pick = pick.astype(bf16)
        high = table.astype(bf16)
        rest = table - high.astype(f32)
        middle, low = split(rest)
        return dot(high, pick) + (dot(middle, pick) + dot(low, pick))

    rate_turned, scale_turned = rate.T, scale.T
    rate_chan_ref[...] = expand(rate_turned, GROUP, groups * GROUP)
    rate_wide = expand(rate_turned, sub, groups * sub)
    scale_wide = expand(scale_turned, sub, groups * sub)
    place = iota((modes, groups * sub), 1) % sub
    back = jnp.where(place == 0, 0, sub - place).astype(f32)
    taps = jnp.sum(scale_wide * jnp.exp(-rate_wide * back), axis=0, keepdims=True)
    ends = scale_wide * jnp.exp(-rate_wide * (sub - 1 - place).astype(f32))
    end_high, end_low = split(ends)
    causal = iota((sub, LANES), 0) >= iota((sub, LANES), 1) % sub
    start = iota((1, LANES), 1) % sub == 0
    mode_pick = iota((modes, each * modes), 0) == iota((modes, each * modes), 1) % modes
    group_at = iota((groups, each * modes), 1) // modes
    ahead = (iota((sub, each * modes), 0) + 1).astype(f32)
    for b in range(blocks):
        for part in range(depth // LANES):
            at = b * depth + part * LANES
            row = taps[:, at : at + LANES]
            row = jnp.where(start, row, pltpu.roll(row, LANES - sub, 1))
            band = pltpu.roll(jnp.broadcast_to(row, (sub, LANES)), 0, 1, stride=1, stride_axis=0)
            high, low = split(jnp.where(causal, band, 0.0))
            to = slice(part * LANES, (part + 1) * LANES)
            left_ref[b, :sub, to] = high
            left_ref[b, sub : 2 * sub, to] = low
        cols = slice(b * depth, (b + 1) * depth)
        left_ref[b, 2 * sub : 2 * sub + modes] = end_high[:, cols]
        left_ref[b, 2 * sub + modes :] = end_low[:, cols]
        spread = jnp.dot(
            (iota((groups, each * modes), 0) == b * each + group_at).astype(f32).T,
            rate,
            precision=lax.Precision.HIGHEST,
            preferred_element_type=f32,
        )
        rate_lane = jnp.sum(jnp.where(mode_pick, spread.T, 0.0), axis=0, keepdims=True)
        high, low = split(jnp.exp(-rate_lane * ahead))
        lag_ref[b, :sub] = jnp.concatenate([high, high], axis=1)
        lag_ref[b, sub:] = jnp.concatenate([low, jnp.zeros_like(low)], axis=1)


def own_groups(rows_each):
    rows = LANES // GROUP * rows_each
    return iota((rows, LANES), 0) // rows_each == iota((rows, LANES), 1) // GROUP


def product_kernel(
    key_ref, value_ref, halo_ref, taps_ref, left_ref, rate_ref, kv_ref, inner_ref, before_ref, state_ref
):
    rows, width = key_ref.shape
    modes = rate_ref.shape[0]
    sub = left_ref.shape[1] // 2 - modes
    count = rows // sub
    halo = halo_ref[...]
    key = featurize(key_ref[...], halo[2:4], taps_ref[1])
    value = featurize(value_ref[...], halo[4:6], taps_ref[2])
    kv = (key * value).astype(bf16)
    kv_ref[...] = kv
    same = own_groups(sub)
    fade = jnp.exp(-rate_ref[...] * float(sub))
    for b in range(width // LANES):
        cols = slice(b * LANES, (b + 1) * LANES)
        total = jnp.zeros((modes, LANES), f32)
        for first in range(0, count, 2):
            right = []
            for s in (first, first + 1):
                piece = kv[s * sub : (s + 1) * sub, cols]
                spread = jnp.concatenate([piece] * (LANES // GROUP), axis=0)
                right.append(jnp.where(same, spread, jnp.zeros_like(spread)))
            out = dot(left_ref[b], jnp.concatenate(right, axis=1))
            for s in (first, first + 1):
                part = out[:, (s - first) * LANES : (s - first + 1) * LANES]
                inner_ref[s * sub : (s + 1) * sub, cols] = part[:sub] + part[sub : 2 * sub]
                before_ref[s * modes : (s + 1) * modes, cols] = total
                total = total * fade[:, cols] + (
                    part[2 * sub : 2 * sub + modes] + part[2 * sub + modes :]
                )
        state_ref[:, cols] = total


def blend_kernel(rows, step, where_ref, state_ref, other_ref, enter_ref, rate_ref, new_ref, into_ref):
    index = where_ref[0]
    upper = (index // step) % 2 == 1
    within = ((index % step) * rows).astype(f32)
    rate = rate_ref[...]
    state, other, enter = state_ref[...], other_ref[...], enter_ref[...]
    into_ref[...] = jnp.where(upper, enter + jnp.exp(-rate * within) * other, enter)
    fade = jnp.exp(-rate * float(step * rows))
    new_ref[...] = jnp.where(upper, other * fade + state, state * fade + other)


def gate_kernel(
    step, where_ref, query_ref, halo_ref, taps_ref, kv_ref, inner_ref, before_ref, enter_ref, other_ref,
    rate_ref, lag_ref, skip_ref, out_ref,
):
    rows, width = query_ref.shape
    modes = rate_ref.shape[0]
    sub = lag_ref.shape[1] // 2
    index = where_ref[0]
    upper = (index // step) % 2 == 1
    within = ((index % step) * rows).astype(f32)
    query = featurize(query_ref[...], halo_ref[0:2], taps_ref[0])
    rate = rate_ref[...]
    enter = enter_ref[...]
    enter = jnp.where(upper, enter + jnp.exp(-rate * within) * other_ref[...], enter)
    fade = jnp.exp(-rate * float(sub))
    same = own_groups(modes)
    for b in range(width // LANES):
        cols = slice(b * LANES, (b + 1) * LANES)
        far = enter[:, cols]
        for first in range(0, rows // sub, 2):
            right = []
            for s in (first, first + 1):
                total = far + before_ref[s * modes : (s + 1) * modes, cols]
                spread = jnp.concatenate([total] * (LANES // GROUP), axis=0)
                right.append(jnp.concatenate(split(jnp.where(same, spread, 0.0)), axis=0))
                far = far * fade[:, cols]
            cross = dot(lag_ref[b], jnp.concatenate(right, axis=1))
            for s in (first, first + 1):
                part = cross[:, (s - first) * LANES : (s - first + 1) * LANES]
                at = slice(s * sub, (s + 1) * sub)
                convolved = inner_ref[at, cols] + (part[:sub] + part[sub:])
                convolved = convolved.astype(bf16).astype(f32)
                kv = kv_ref[at, cols].astype(f32)
                out_ref[at, cols] = (query[at, cols] * (convolved + skip_ref[:, cols] * kv)).astype(bf16)


def prepare_kernel(which_ref, query_ref, key_ref, value_ref, weight_ref, tail_ref, piece_ref, rows_ref, sems):
    keep = FEAT - 1
    height = rows_ref.shape[1]
    width = piece_ref.shape[1]
    at = pl.multiple_of(which_ref[0] * width, width)
    copies = [pltpu.make_async_copy(weight_ref.at[:, pl.ds(at, width)], piece_ref, sems.at[3])]
    for i, ref in enumerate((query_ref, key_ref, value_ref)):
        first = ref.shape[0] - height
        copies.append(
            pltpu.make_async_copy(ref.at[pl.ds(first, height)], rows_ref.at[i], sems.at[i])
        )
    for copy in copies:
        copy.start()
    for copy in copies[1:]:
        copy.wait()
    for i in range(3):
        tail_ref[i * keep : (i + 1) * keep] = rows_ref[i].astype(f32)[height - keep :]
    tail_ref[3 * keep :] = jnp.zeros((tail_ref.shape[0] - 3 * keep, tail_ref.shape[1]), f32)
    copies[0].wait()


def prepare(query, key, value, weight):
    chans = query.shape[1]
    depth, cols = weight.shape
    which = (lax.axis_index("ctx") % 8)[None].astype(jnp.int32)
    hbm = pl.BlockSpec(memory_space=pltpu.HBM)
    vmem = pl.BlockSpec(memory_space=pltpu.VMEM)
    return pl.pallas_call(
        prepare_kernel,
        in_specs=[pl.BlockSpec(memory_space=pltpu.SMEM)] + [hbm] * 4,
        out_specs=[vmem, vmem],
        out_shape=[
            jax.ShapeDtypeStruct((8, chans), f32),
            jax.ShapeDtypeStruct((depth, cols // 8), bf16),
        ],
        scratch_shapes=[pltpu.VMEM((3, 16, chans), bf16), pltpu.SemaphoreType.DMA((4,))],
        compiler_params=params(63 << 20),
        name="prepare",
    )(which, query, key, value, weight)


def conv_path(query, key, value, halo, near, taps, rate, residues, skip):
    rows, chans = query.shape
    groups, modes = rate.shape
    count = lax.axis_size("ctx")
    here = lax.axis_index("ctx")[None].astype(jnp.int32)
    blocks = chans // LANES
    depth = LANES // GROUP * SUB
    steps = chans // WIDE
    per = WIDE // LANES
    vmem = pl.BlockSpec(memory_space=pltpu.VMEM)
    smem = pl.BlockSpec(memory_space=pltpu.SMEM)
    state_shape = jax.ShapeDtypeStruct((modes, chans), f32)
    left, lag, rate_chan = pl.pallas_call(
        table_kernel,
        in_specs=[vmem, vmem],
        out_specs=[vmem] * 3,
        out_shape=[
            jax.ShapeDtypeStruct((blocks, 2 * (SUB + modes), depth), bf16),
            jax.ShapeDtypeStruct((blocks, 2 * SUB, 2 * (LANES // GROUP) * modes), bf16),
            state_shape,
        ],
        compiler_params=params(),
        name="tables",
    )(rate, residues)
    near = after(near, halo, left)
    near_one, near_two = hop(near, True), hop(near, False)

    def wide(height):
        return pl.BlockSpec((height, WIDE), lambda b: (0, b))

    def stack(array):
        return pl.BlockSpec((per,) + array.shape[1:], lambda b: (b, 0, 0))

    taps_spec = pl.BlockSpec((3, FEAT, WIDE), lambda b: (0, 0, b))
    subs = rows // SUB
    kv, inner, before, state = pl.pallas_call(
        product_kernel,
        grid=(steps,),
        in_specs=[wide(rows), wide(rows), wide(8), taps_spec, stack(left), wide(modes)],
        out_specs=[wide(rows), wide(rows), wide(subs * modes), wide(modes)],
        out_shape=[
            jax.ShapeDtypeStruct((rows, chans), bf16),
            jax.ShapeDtypeStruct((rows, chans), f32),
            jax.ShapeDtypeStruct((subs * modes, chans), f32),
            state_shape,
        ],
        compiler_params=params(),
        name="kv_and_state",
    )(key, value, halo, taps, left, rate_chan)
    enter = jnp.zeros_like(state)
    step = 1
    states = [state]
    while True:
        other = lax.ppermute(state, "ctx", [(i, i ^ step) for i in range(count)])
        if 2 * step >= count:
            break
        state, enter = pl.pallas_call(
            functools.partial(blend_kernel, rows, step),
            in_specs=[smem] + [vmem] * 4,
            out_specs=[vmem] * 2,
            out_shape=[state_shape] * 2,
            compiler_params=params(),
            name="blend_states",
        )(here, state, other, enter, rate_chan)
        step *= 2
        states.append(state)
    gated = pl.pallas_call(
        functools.partial(gate_kernel, step),
        grid=(steps,),
        in_specs=[
            smem,
            wide(rows),
            wide(8),
            taps_spec,
            wide(rows),
            wide(rows),
            wide(subs * modes),
            wide(modes),
            wide(modes),
            wide(modes),
            stack(lag),
            wide(1),
        ],
        out_specs=wide(rows),
        out_shape=jax.ShapeDtypeStruct((rows, chans), bf16),
        compiler_params=params(),
        name="gate",
    )(here, query, halo, taps, kv, inner, before, enter, other, rate_chan, lag, skip[None])
    return gated, states, (near, near_one, near_two)


def hop(x, first):
    count = lax.axis_size("ctx")
    even, odd = (2, 4) if first else (4, 2)
    return lax.ppermute(x, "ctx", [(i, i ^ (odd if i % 2 else even)) for i in range(count)])


def send_weight(mine):
    near = lax.ppermute(mine, "fsdp", [(i, i ^ 1) for i in range(4)])
    two = lax.ppermute(mine, "fsdp", [(i, i ^ 2) for i in range(4)])
    three = lax.ppermute(after(mine, near), "fsdp", [(i, i ^ 3) for i in range(4)])
    return near, two, three


def spread_weight(near, two, three, states):
    near, one, side = near
    corner = hop(after(one, states[1]), False)
    slot_one = (near, one, side, corner)
    two = after(two, states[1])
    one, side = hop(two, True), hop(two, False)
    corner = hop(after(one, states[-1]), False)
    slot_two = (two, one, side, corner)
    three = after(three, states[-1])
    one, side = hop(three, True), hop(three, False)
    corner = hop(after(one, *slot_two), False)
    return slot_one, slot_two, (three, one, side, corner)


def matmul_kernel(slot_count, has_own, has_acc, last, nums_ref, *refs):
    refs = list(refs)
    mine_ref, other_ref = refs[0], refs[1]
    refs = refs[2:]
    if has_own:
        weight_ref = refs.pop(0)
    slots = [refs[4 * s : 4 * s + 4] for s in range(slot_count)]
    refs = refs[4 * slot_count :]
    if has_acc:
        acc_ref = refs.pop(0)
    rows = mine_ref.shape[0]
    depth, block = slots[0][0].shape

    def rows_of(part):
        at = pl.multiple_of(nums_ref[part] * depth, depth)
        return jnp.concatenate(
            [mine_ref[:, pl.ds(at, depth)], other_ref[:, pl.ds(at, depth)]], axis=0
        )

    lhs = [rows_of(1 + s) for s in range(slot_count)]
    if has_own:
        own = rows_of(0)
    for r in range(4):
        total = acc_ref[:, r * block : (r + 1) * block] if has_acc else None
        if has_own:
            at = pl.multiple_of(nums_ref[4 + r] * block, block)
            total = dot(own, weight_ref[:, pl.ds(at, block)])
        for s in range(slot_count):
            part = dot(lhs[s], slots[s][r][...])
            total = part if total is None else total + part
        if last:
            at = pl.multiple_of(nums_ref[8 + r] * block, block)
            done = total.astype(bf16)
            refs[0][:, pl.ds(at, block)] = done[:rows]
            refs[1][:, pl.ds(at, block)] = done[rows:]
        else:
            refs[0][:, r * block : (r + 1) * block] = total


def join_kernel(nums_ref, mine_ref, other_ref, out_ref):
    block = mine_ref.shape[1] // 4
    core = nums_ref[0]
    for h in range(4):
        at = pl.multiple_of((2 * h + core) * block, block)
        out_ref[:, pl.ds(at, block)] = mine_ref[:, h * block : (h + 1) * block]
        at = pl.multiple_of((2 * h + 1 - core) * block, block)
        out_ref[:, pl.ds(at, block)] = other_ref[:, h * block : (h + 1) * block]


def project(gated, weight, slots):
    count = lax.axis_size("ctx")
    index = lax.axis_index("ctx")
    place = lax.axis_index("fsdp")
    rows = gated.shape[0]
    depth, cols = weight.shape
    half = cols // 2
    swap = [(i, i ^ 1) for i in range(count)]
    other = lax.ppermute(gated, "ctx", swap)
    core = index % 2
    first, second = jnp.where(core == 0, 2, 4), jnp.where(core == 0, 4, 2)
    rel = index % 8
    order = [rel, rel ^ first, rel ^ second, rel ^ 6]
    parts = [place, place ^ 1, place ^ 2, place ^ 3]
    nums = jnp.stack(parts + order + [n // 2 for n in order]).astype(jnp.int32)
    vmem = pl.BlockSpec(memory_space=pltpu.VMEM)
    smem = pl.BlockSpec(memory_space=pltpu.SMEM)
    acc = pl.pallas_call(
        functools.partial(matmul_kernel, 2, True, False, False),
        in_specs=[smem] + [vmem] * 11,
        out_specs=vmem,
        out_shape=jax.ShapeDtypeStruct((2 * rows, half), f32),
        compiler_params=params(),
        name="project_near",
    )(nums, gated, other, weight, *slots[0], *slots[1])
    late = nums.at[1].set(nums[3])
    mine, theirs = pl.pallas_call(
        functools.partial(matmul_kernel, 1, False, True, True),
        in_specs=[smem] + [vmem] * 7,
        out_specs=[vmem, vmem],
        out_shape=[jax.ShapeDtypeStruct((rows, half), bf16)] * 2,
        compiler_params=params(),
        name="project_far",
    )(late, gated, other, *slots[2], acc)
    back = lax.ppermute(theirs, "ctx", swap)
    return pl.pallas_call(
        join_kernel,
        in_specs=[smem, vmem, vmem],
        out_specs=vmem,
        out_shape=jax.ShapeDtypeStruct((rows, cols), bf16),
        compiler_params=params(),
        name="join_columns",
    )(core[None].astype(jnp.int32), mine, back)


def local(query_in, key_in, value_in, feature_taps, decay_rate, residues, skip_gain, out_weight):
    query, key, value = query_in[0], key_in[0], value_in[0]
    tails, mine = prepare(query, key, value, out_weight)
    count = lax.axis_size("ctx")
    halo = lax.ppermute(tails, "ctx", [(i, i + 1) for i in range(count - 1)])
    near, two, three = send_weight(mine)
    gated, states, near = conv_path(
        query, key, value, halo, near, feature_taps, decay_rate, residues, skip_gain
    )
    return project(gated, out_weight, spread_weight(near, two, three, states))[None]


def solution(mesh):
    return jax.shard_map(
        local,
        mesh=mesh,
        in_specs=(
            P("fsdp", "ctx", None),
            P("fsdp", "ctx", None),
            P("fsdp", "ctx", None),
            P(),
            P(),
            P(),
            P(),
            P("fsdp", None),
        ),
        out_specs=P("fsdp", "ctx", None),
        check_vma=False,
    )
```

```python
import functools

import jax
import jax.numpy as jnp
from jax import lax
from jax.experimental import pallas as pl
from jax.experimental.pallas import tpu as pltpu
from jax.sharding import PartitionSpec as P

GROUP = 16
HOLD = [[], [], [], []]
RELAY = {'z1': [], 'a1': ['s1'], 'mine': ['z1'], 'z2': ['s1'], 'z3': ['s2'], 'a3': []}
FEAT = 3
WIDE = 512
LANES = 128
SUB = 32
VMEM_LIMIT = 48 << 20
PREP = 63
COST = pl.CostEstimate(flops=0, bytes_accessed=0, transcendentals=0)

bf16 = jnp.bfloat16
f32 = jnp.float32


def waiting(kernel, count, first):
    def body(*refs):
        kernel(*refs[:first], *refs[first + count :])

    return body


def params(limit=VMEM_LIMIT):
    return pltpu.CompilerParams(vmem_limit_bytes=limit)


def split(x):
    high = x.astype(bf16)
    return high, (x - high.astype(f32)).astype(bf16)


def iota(shape, dim):
    return lax.broadcasted_iota(jnp.int32, shape, dim)


def one_less_exp(x):
    small = jnp.minimum(x, 0.5)
    series = jnp.ones_like(x)
    for n in range(9, 1, -1):
        series = 1.0 - small * (1.0 / n) * series
    return jnp.where(x < 0.5, small * series, 1.0 - jnp.exp(-x))


def dot(a, b):
    return jnp.dot(a, b, preferred_element_type=f32)


def featurize(rows, tail, taps):
    values = rows.astype(f32)
    at = iota(values.shape, 0)
    one = jnp.where(at == 0, tail[1:2], pltpu.roll(values, 1, 0))
    two = jnp.where(at == 0, tail[0:1], jnp.where(at == 1, tail[1:2], pltpu.roll(values, 2, 0)))
    return taps[0:1] * values + taps[1:2] * one + taps[2:3] * two


def table_kernel(rate_ref, residue_ref, left_ref, lag_ref, rate_chan_ref):
    rate = rate_ref[...]
    groups, modes = rate.shape
    scale = residue_ref[...] * jnp.sqrt(one_less_exp(2.0 * rate))
    blocks, _, depth = left_ref.shape
    sub = left_ref.shape[1] // 2 - modes
    each = groups // blocks

    def expand(table, width, count):
        pick = iota((groups, count), 0) == iota((groups, count), 1) // width
        pick = pick.astype(bf16)
        high = table.astype(bf16)
        rest = table - high.astype(f32)
        middle, low = split(rest)
        return dot(high, pick) + (dot(middle, pick) + dot(low, pick))

    rate_turned, scale_turned = rate.T, scale.T
    rate_chan_ref[...] = expand(rate_turned, GROUP, groups * GROUP)
    rate_wide = expand(rate_turned, sub, groups * sub)
    scale_wide = expand(scale_turned, sub, groups * sub)
    place = iota((modes, groups * sub), 1) % sub
    back = jnp.where(place == 0, 0, sub - place).astype(f32)
    taps = jnp.sum(scale_wide * jnp.exp(-rate_wide * back), axis=0, keepdims=True)
    ends = scale_wide * jnp.exp(-rate_wide * (sub - 1 - place).astype(f32))
    end_high, end_low = split(ends)
    causal = iota((sub, LANES), 0) >= iota((sub, LANES), 1) % sub
    start = iota((1, LANES), 1) % sub == 0
    mode_pick = iota((modes, each * modes), 0) == iota((modes, each * modes), 1) % modes
    group_at = iota((groups, each * modes), 1) // modes
    ahead = (iota((sub, each * modes), 0) + 1).astype(f32)
    for b in range(blocks):
        for part in range(depth // LANES):
            at = b * depth + part * LANES
            row = taps[:, at : at + LANES]
            row = jnp.where(start, row, pltpu.roll(row, LANES - sub, 1))
            band = pltpu.roll(jnp.broadcast_to(row, (sub, LANES)), 0, 1, stride=1, stride_axis=0)
            high, low = split(jnp.where(causal, band, 0.0))
            to = slice(part * LANES, (part + 1) * LANES)
            left_ref[b, :sub, to] = high
            left_ref[b, sub : 2 * sub, to] = low
        cols = slice(b * depth, (b + 1) * depth)
        left_ref[b, 2 * sub : 2 * sub + modes] = end_high[:, cols]
        left_ref[b, 2 * sub + modes :] = end_low[:, cols]
        spread = jnp.dot(
            (iota((groups, each * modes), 0) == b * each + group_at).astype(f32).T,
            rate,
            precision=lax.Precision.HIGHEST,
            preferred_element_type=f32,
        )
        rate_lane = jnp.sum(jnp.where(mode_pick, spread.T, 0.0), axis=0, keepdims=True)
        high, low = split(jnp.exp(-rate_lane * ahead))
        lag_ref[b, :sub] = jnp.concatenate([high, high], axis=1)
        lag_ref[b, sub:] = jnp.concatenate([low, jnp.zeros_like(low)], axis=1)


def own_groups(rows_each):
    rows = LANES // GROUP * rows_each
    return iota((rows, LANES), 0) // rows_each == iota((rows, LANES), 1) // GROUP


def product_kernel(
    key_ref, value_ref, halo_ref, taps_ref, left_ref, rate_ref, kv_ref, inner_ref, before_ref, state_ref
):
    rows, width = key_ref.shape
    modes = rate_ref.shape[0]
    sub = left_ref.shape[1] // 2 - modes
    count = rows // sub
    halo = halo_ref[...]
    key = featurize(key_ref[...], halo[2:4], taps_ref[1])
    value = featurize(value_ref[...], halo[4:6], taps_ref[2])
    kv = (key * value).astype(bf16)
    kv_ref[...] = kv
    same = own_groups(sub)
    fade = jnp.exp(-rate_ref[...] * float(sub))
    for b in range(width // LANES):
        cols = slice(b * LANES, (b + 1) * LANES)
        total = jnp.zeros((modes, LANES), f32)
        for first in range(0, count, 2):
            right = []
            for s in (first, first + 1):
                piece = kv[s * sub : (s + 1) * sub, cols]
                spread = jnp.concatenate([piece] * (LANES // GROUP), axis=0)
                right.append(jnp.where(same, spread, jnp.zeros_like(spread)))
            out = dot(left_ref[b], jnp.concatenate(right, axis=1))
            for s in (first, first + 1):
                part = out[:, (s - first) * LANES : (s - first + 1) * LANES]
                inner_ref[s * sub : (s + 1) * sub, cols] = part[:sub] + part[sub : 2 * sub]
                before_ref[s * modes : (s + 1) * modes, cols] = total
                total = total * fade[:, cols] + (
                    part[2 * sub : 2 * sub + modes] + part[2 * sub + modes :]
                )
        state_ref[:, cols] = total


def blend_kernel(rows, step, where_ref, state_ref, other_ref, enter_ref, rate_ref, new_ref, into_ref):
    index = where_ref[0]
    upper = (index // step) % 2 == 1
    within = ((index % step) * rows).astype(f32)
    rate = rate_ref[...]
    state, other, enter = state_ref[...], other_ref[...], enter_ref[...]
    into_ref[...] = jnp.where(upper, enter + jnp.exp(-rate * within) * other, enter)
    fade = jnp.exp(-rate * float(step * rows))
    new_ref[...] = jnp.where(upper, other * fade + state, state * fade + other)


def gate_kernel(
    step, where_ref, query_ref, halo_ref, taps_ref, kv_ref, inner_ref, before_ref, enter_ref, other_ref,
    rate_ref, lag_ref, skip_ref, out_ref,
):
    rows, width = query_ref.shape
    modes = rate_ref.shape[0]
    sub = lag_ref.shape[1] // 2
    index = where_ref[0]
    upper = (index // step) % 2 == 1
    within = ((index % step) * rows).astype(f32)
    query = featurize(query_ref[...], halo_ref[0:2], taps_ref[0])
    rate = rate_ref[...]
    enter = enter_ref[...]
    enter = jnp.where(upper, enter + jnp.exp(-rate * within) * other_ref[...], enter)
    fade = jnp.exp(-rate * float(sub))
    same = own_groups(modes)
    for b in range(width // LANES):
        cols = slice(b * LANES, (b + 1) * LANES)
        far = enter[:, cols]
        for first in range(0, rows // sub, 2):
            right = []
            for s in (first, first + 1):
                total = far + before_ref[s * modes : (s + 1) * modes, cols]
                spread = jnp.concatenate([total] * (LANES // GROUP), axis=0)
                right.append(jnp.concatenate(split(jnp.where(same, spread, 0.0)), axis=0))
                far = far * fade[:, cols]
            cross = dot(lag_ref[b], jnp.concatenate(right, axis=1))
            for s in (first, first + 1):
                part = cross[:, (s - first) * LANES : (s - first + 1) * LANES]
                at = slice(s * sub, (s + 1) * sub)
                convolved = inner_ref[at, cols] + (part[:sub] + part[sub:])
                convolved = convolved.astype(bf16).astype(f32)
                kv = kv_ref[at, cols].astype(f32)
                out_ref[at, cols] = (query[at, cols] * (convolved + skip_ref[:, cols] * kv)).astype(bf16)


def prepare_kernel(which_ref, query_ref, key_ref, value_ref, weight_ref, tail_ref, piece_ref, rows_ref, sems):
    keep = FEAT - 1
    height = rows_ref.shape[1]
    width = piece_ref.shape[1]
    at = pl.multiple_of((which_ref[0] & 7) * width, width)
    copies = [pltpu.make_async_copy(weight_ref.at[:, pl.ds(at, width)], piece_ref, sems.at[3])]
    for i, ref in enumerate((query_ref, key_ref, value_ref)):
        first = ref.shape[0] - height
        copies.append(
            pltpu.make_async_copy(ref.at[pl.ds(first, height)], rows_ref.at[i], sems.at[i])
        )
    for copy in copies:
        copy.start()
    for copy in copies[1:]:
        copy.wait()
    for i in range(3):
        tail_ref[i * keep : (i + 1) * keep] = rows_ref[i].astype(f32)[height - keep :]
    tail_ref[3 * keep :] = jnp.zeros((tail_ref.shape[0] - 3 * keep, tail_ref.shape[1]), f32)
    copies[0].wait()


def prepare(query, key, value, weight):
    chans = query.shape[1]
    depth, cols = weight.shape
    which = lax.axis_index("ctx")[None].astype(jnp.int32)
    hbm = pl.BlockSpec(memory_space=pltpu.HBM)
    vmem = pl.BlockSpec(memory_space=pltpu.VMEM)
    return pl.pallas_call(
        prepare_kernel,
        in_specs=[pl.BlockSpec(memory_space=pltpu.SMEM)] + [hbm] * 4,
        out_specs=[vmem, vmem],
        out_shape=[
            jax.ShapeDtypeStruct((8, chans), f32),
            jax.ShapeDtypeStruct((depth, cols // 8), bf16),
        ],
        scratch_shapes=[pltpu.VMEM((3, 16, chans), bf16), pltpu.SemaphoreType.DMA((4,))],
        compiler_params=params(PREP << 20),
        name="prepare",
    )(which, query, key, value, weight)


def relay_kernel(in_ref, *refs):
    del in_ref, refs


def relay(x, *held):
    unused = pl.BlockSpec(memory_space=pl.ANY)
    return pl.pallas_call(
        relay_kernel,
        in_specs=[unused] * (1 + len(held)),
        out_specs=unused,
        out_shape=jax.ShapeDtypeStruct(x.shape, x.dtype),
        input_output_aliases={0: 0},
        compiler_params=params(),
        cost_estimate=COST,
        name="relay",
    )(x, *held)


def conv_path(query, key, value, halo, near, two, mine, rate, residues, taps, skip):
    rows, chans = query.shape
    groups, modes = rate.shape
    blocks = chans // LANES
    depth = LANES // GROUP * SUB
    count = lax.axis_size("ctx")
    here = lax.axis_index("ctx")[None].astype(jnp.int32)
    steps = chans // WIDE
    per = WIDE // LANES
    vmem = pl.BlockSpec(memory_space=pltpu.VMEM)
    smem = pl.BlockSpec(memory_space=pltpu.SMEM)
    state_shape = jax.ShapeDtypeStruct((modes, chans), f32)
    left, lag, rate_chan = pl.pallas_call(
        table_kernel,
        in_specs=[vmem, vmem],
        out_specs=[vmem] * 3,
        out_shape=[
            jax.ShapeDtypeStruct((blocks, 2 * (SUB + modes), depth), bf16),
            jax.ShapeDtypeStruct((blocks, 2 * SUB, 2 * (LANES // GROUP) * modes), bf16),
            state_shape,
        ],
        compiler_params=params(),
        cost_estimate=COST,
        name="tables",
    )(rate, residues)

    def wide(height):
        return pl.BlockSpec((height, WIDE), lambda b: (0, b))

    def stack(array):
        return pl.BlockSpec((per,) + array.shape[1:], lambda b: (b, 0, 0))

    taps_spec = pl.BlockSpec((3, FEAT, WIDE), lambda b: (0, 0, b))
    subs = rows // SUB
    unused = pl.BlockSpec(memory_space=pl.ANY)
    pieces = dict(z1=near, z2=two)
    held = [pieces[n] for n in HOLD[0]]
    kv, inner, before, state = pl.pallas_call(
        waiting(product_kernel, len(held), 6),
        grid=(steps,),
        in_specs=[wide(rows), wide(rows), wide(8), taps_spec, stack(left), wide(modes)] + [unused] * len(held),
        out_specs=[wide(rows), wide(rows), wide(subs * modes), wide(modes)],
        out_shape=[
            jax.ShapeDtypeStruct((rows, chans), bf16),
            jax.ShapeDtypeStruct((rows, chans), f32),
            jax.ShapeDtypeStruct((subs * modes, chans), f32),
            state_shape,
        ],
        compiler_params=params(),
        cost_estimate=COST,
        name="kv_and_state",
    )(key, value, halo, taps, left, rate_chan, *held)
    enter = jnp.zeros_like(state)
    pieces["k"] = state
    step = 1
    at = lambda array, name: relay(array, *[pieces[n] for n in RELAY[name]]) if RELAY[name] else array
    while True:
        if step == 1:
            near = at(near, "z1")
            pieces["a1"], pieces["b1"] = hop(near, True), hop(near, False)
        other = lax.ppermute(state, "ctx", [(i, i ^ step) for i in range(count)])
        if 2 * step >= count:
            break
        held = [pieces[n] for n in HOLD[1 if step == 1 else 2]]
        state, enter = pl.pallas_call(
            waiting(functools.partial(blend_kernel, rows, step), len(held), 5),
            in_specs=[smem] + [vmem] * 4 + [unused] * len(held),
            out_specs=[vmem] * 2,
            out_shape=[state_shape] * 2,
            compiler_params=params(),
            cost_estimate=COST,
            name="blend_states",
        )(here, state, other, enter, rate_chan, *held)
        if step == 1:
            pieces["s1"] = state
            pieces["c1"] = hop(at(pieces["a1"], "a1"), False)
            three = lax.ppermute(at(mine, "mine"), "fsdp", [(i, i ^ 3) for i in range(4)])
            pieces["z3"] = three
        if step == 2:
            pieces["s2"] = state
            two = at(two, "z2")
            pieces["a2"], pieces["b2"] = hop(two, True), hop(two, False)
            pieces["c2"] = hop(pieces["a2"], False)
        step *= 2
    pieces["y"] = other
    three = at(three, "z3")
    pieces["a3"], pieces["b3"] = hop(three, True), hop(three, False)
    pieces["c3"] = hop(at(pieces["a3"], "a3"), False)
    held = [pieces[n] for n in HOLD[3]]
    slots = [
        [first] + [pieces[n + i] for n in "abc"] for first, i in ((near, "1"), (two, "2"), (three, "3"))
    ]
    gated = pl.pallas_call(
        waiting(functools.partial(gate_kernel, step), len(held), 12),
        grid=(steps,),
        in_specs=[
            smem,
            wide(rows),
            wide(8),
            taps_spec,
            wide(rows),
            wide(rows),
            wide(subs * modes),
            wide(modes),
            wide(modes),
            wide(modes),
            stack(lag),
            wide(1),
        ]
        + [unused] * len(held),
        out_specs=wide(rows),
        out_shape=jax.ShapeDtypeStruct((rows, chans), bf16),
        compiler_params=params(),
        cost_estimate=COST,
        name="gate",
    )(here, query, halo, taps, kv, inner, before, enter, other, rate_chan, lag, skip[None], *held)
    return gated, slots


def hop(x, first):
    count = lax.axis_size("ctx")
    even, odd = (2, 4) if first else (4, 2)
    return lax.ppermute(x, "ctx", [(i, i ^ (odd if i % 2 else even)) for i in range(count)])


def block_order(index):
    core = index & 1
    block = index & 7
    return [block, block ^ (2 + 2 * core), block ^ (4 - 2 * core), block ^ 6]


def both_rows(mine_ref, other_ref, part, depth):
    at = pl.ds(pl.multiple_of(part * depth, depth), depth)
    return jnp.concatenate([mine_ref[:, at], other_ref[:, at]], axis=0)


def near_kernel(index_ref, place_ref, mine_ref, other_ref, weight_ref, *refs):
    index, place = index_ref[0], place_ref[0]
    one, two, acc_ref = refs[:4], refs[4:8], refs[8]
    depth, block = one[0].shape
    own, left_one, left_two = [both_rows(mine_ref, other_ref, place ^ n, depth) for n in (0, 1, 2)]
    for r, at in enumerate(block_order(index)):
        total = dot(own, weight_ref[:, pl.ds(pl.multiple_of(at * block, block), block)])
        total = total + dot(left_one, one[r][...]) + dot(left_two, two[r][...])
        acc_ref[:, r * block : (r + 1) * block] = total


def far_kernel(index_ref, place_ref, mine_ref, other_ref, *refs):
    index, place = index_ref[0], place_ref[0]
    three, acc_ref, own_ref, out_ref = refs[:4], refs[4], refs[5], refs[6]
    depth, block = three[0].shape
    rows = mine_ref.shape[0]
    left = both_rows(mine_ref, other_ref, place ^ 3, depth)
    for r, at in enumerate(block_order(index)):
        total = acc_ref[:, r * block : (r + 1) * block] + dot(left, three[r][...])
        total = total.astype(bf16)
        cols = pl.ds(pl.multiple_of((at >> 1) * block, block), block)
        own_ref[:, cols] = total[:rows]
        out_ref[:, cols] = total[rows:]


def join_kernel(nums_ref, mine_ref, other_ref, out_ref):
    block = mine_ref.shape[1] // 4
    core = nums_ref[0] & 1
    for h in range(4):
        at = pl.multiple_of((2 * h + core) * block, block)
        out_ref[:, pl.ds(at, block)] = mine_ref[:, h * block : (h + 1) * block]
        at = pl.multiple_of((2 * h + 1 - core) * block, block)
        out_ref[:, pl.ds(at, block)] = other_ref[:, h * block : (h + 1) * block]


def project(gated, weight, slots):
    count = lax.axis_size("ctx")
    index = lax.axis_index("ctx")[None].astype(jnp.int32)
    place = lax.axis_index("fsdp")[None].astype(jnp.int32)
    rows = gated.shape[0]
    cols = weight.shape[1]
    swap = [(i, i ^ 1) for i in range(count)]
    other = lax.ppermute(gated, "ctx", swap)
    vmem = pl.BlockSpec(memory_space=pltpu.VMEM)
    smem = pl.BlockSpec(memory_space=pltpu.SMEM)

    def call(kernel, name, shapes, scalars, *args):
        return pl.pallas_call(
            kernel,
            in_specs=[smem] * len(scalars) + [vmem] * len(args),
            out_specs=[vmem] * len(shapes),
            out_shape=shapes,
            compiler_params=params(),
            cost_estimate=COST,
            name=name,
        )(*scalars, *args)

    (acc,) = call(
        near_kernel,
        "project_near",
        [jax.ShapeDtypeStruct((2 * rows, cols // 2), f32)],
        (index, place), gated, other, weight, *slots[0], *slots[1],
    )
    mine, theirs = call(
        far_kernel,
        "project_far",
        [jax.ShapeDtypeStruct((rows, cols // 2), bf16)] * 2,
        (index, place), gated, other, *slots[2], acc,
    )
    back = lax.ppermute(theirs, "ctx", swap)
    (out,) = call(
        join_kernel,
        "join_columns",
        [jax.ShapeDtypeStruct((rows, cols), bf16)],
        (index,), mine, back,
    )
    return out


def local(query_in, key_in, value_in, feature_taps, decay_rate, residues, skip_gain, out_weight):
    query, key, value = query_in[0], key_in[0], value_in[0]
    tails, mine = prepare(query, key, value, out_weight)
    count = lax.axis_size("ctx")
    halo = lax.ppermute(tails, "ctx", [(i, i + 1) for i in range(count - 1)])
    near = lax.ppermute(mine, "fsdp", [(i, i ^ 1) for i in range(4)])
    two = lax.ppermute(mine, "fsdp", [(i, i ^ 2) for i in range(4)])
    gated, slots = conv_path(
        query, key, value, halo, near, two, mine, decay_rate, residues, feature_taps, skip_gain
    )
    return project(gated, out_weight, slots)[None]


def solution(mesh):
    return jax.shard_map(
        local,
        mesh=mesh,
        in_specs=(
            P("fsdp", "ctx", None),
            P("fsdp", "ctx", None),
            P("fsdp", "ctx", None),
            P(),
            P(),
            P(),
            P(),
            P("fsdp", None),
        ),
        out_specs=P("fsdp", "ctx", None),
        check_vma=False,
    )
```

```python
import functools

import jax
import jax.numpy as jnp
from jax import lax
from jax.experimental import pallas as pl
from jax.experimental.pallas import tpu as pltpu
from jax.sharding import PartitionSpec as P

GROUP = 16
HOLD = [[], [], [], []]
RELAY = {'z1': [], 'a1': [], 'mine': ['z1'], 'z2': ['s1'], 'z3': ['s2'], 'a3': []}
FEAT = 3
WIDE = 512
LANES = 128
SUB = 32
VMEM_LIMIT = 48 << 20
PREP = 61
COST = pl.CostEstimate(flops=0, bytes_accessed=0, transcendentals=0)

bf16 = jnp.bfloat16
f32 = jnp.float32


def waiting(kernel, count, first):
    def body(*refs):
        kernel(*refs[:first], *refs[first + count :])

    return body


def params(limit=VMEM_LIMIT):
    return pltpu.CompilerParams(vmem_limit_bytes=limit)


def split(x):
    high = x.astype(bf16)
    return high, (x - high.astype(f32)).astype(bf16)


def iota(shape, dim):
    return lax.broadcasted_iota(jnp.int32, shape, dim)


def one_less_exp(x):
    small = jnp.minimum(x, 0.5)
    series = jnp.ones_like(x)
    for n in range(9, 1, -1):
        series = 1.0 - small * (1.0 / n) * series
    return jnp.where(x < 0.5, small * series, 1.0 - jnp.exp(-x))


def dot(a, b):
    return jnp.dot(a, b, preferred_element_type=f32)


def featurize(rows, tail, taps):
    values = rows.astype(f32)
    at = iota(values.shape, 0)
    one = jnp.where(at == 0, tail[1:2], pltpu.roll(values, 1, 0))
    two = jnp.where(at == 0, tail[0:1], jnp.where(at == 1, tail[1:2], pltpu.roll(values, 2, 0)))
    return taps[0:1] * values + taps[1:2] * one + taps[2:3] * two


def table_kernel(rate_ref, residue_ref, left_ref, lag_ref, rate_chan_ref):
    rate = rate_ref[...]
    groups, modes = rate.shape
    scale = residue_ref[...] * jnp.sqrt(one_less_exp(2.0 * rate))
    blocks, _, depth = left_ref.shape
    sub = left_ref.shape[1] // 2 - modes
    each = groups // blocks

    def expand(table, width, count):
        pick = iota((groups, count), 0) == iota((groups, count), 1) // width
        pick = pick.astype(bf16)
        high = table.astype(bf16)
        rest = table - high.astype(f32)
        middle, low = split(rest)
        return dot(high, pick) + (dot(middle, pick) + dot(low, pick))

    rate_turned, scale_turned = rate.T, scale.T
    rate_chan_ref[...] = expand(rate_turned, GROUP, groups * GROUP)
    rate_wide = expand(rate_turned, sub, groups * sub)
    scale_wide = expand(scale_turned, sub, groups * sub)
    place = iota((modes, groups * sub), 1) % sub
    back = jnp.where(place == 0, 0, sub - place).astype(f32)
    taps = jnp.sum(scale_wide * jnp.exp(-rate_wide * back), axis=0, keepdims=True)
    ends = scale_wide * jnp.exp(-rate_wide * (sub - 1 - place).astype(f32))
    end_high, end_low = split(ends)
    causal = iota((sub, LANES), 0) >= iota((sub, LANES), 1) % sub
    start = iota((1, LANES), 1) % sub == 0
    mode_pick = iota((modes, each * modes), 0) == iota((modes, each * modes), 1) % modes
    group_at = iota((groups, each * modes), 1) // modes
    ahead = (iota((sub, each * modes), 0) + 1).astype(f32)
    for b in range(blocks):
        for part in range(depth // LANES):
            at = b * depth + part * LANES
            row = taps[:, at : at + LANES]
            row = jnp.where(start, row, pltpu.roll(row, LANES - sub, 1))
            band = pltpu.roll(jnp.broadcast_to(row, (sub, LANES)), 0, 1, stride=1, stride_axis=0)
            high, low = split(jnp.where(causal, band, 0.0))
            to = slice(part * LANES, (part + 1) * LANES)
            left_ref[b, :sub, to] = high
            left_ref[b, sub : 2 * sub, to] = low
        cols = slice(b * depth, (b + 1) * depth)
        left_ref[b, 2 * sub : 2 * sub + modes] = end_high[:, cols]
        left_ref[b, 2 * sub + modes :] = end_low[:, cols]
        spread = jnp.dot(
            (iota((groups, each * modes), 0) == b * each + group_at).astype(f32).T,
            rate,
            precision=lax.Precision.HIGHEST,
            preferred_element_type=f32,
        )
        rate_lane = jnp.sum(jnp.where(mode_pick, spread.T, 0.0), axis=0, keepdims=True)
        high, low = split(jnp.exp(-rate_lane * ahead))
        lag_ref[b, :sub] = jnp.concatenate([high, high], axis=1)
        lag_ref[b, sub:] = jnp.concatenate([low, jnp.zeros_like(low)], axis=1)


def own_groups(rows_each):
    rows = LANES // GROUP * rows_each
    return iota((rows, LANES), 0) // rows_each == iota((rows, LANES), 1) // GROUP


def product_kernel(
    key_ref, value_ref, halo_ref, taps_ref, left_ref, rate_ref, kv_ref, inner_ref, before_ref, state_ref
):
    rows, width = key_ref.shape
    modes = rate_ref.shape[0]
    sub = left_ref.shape[1] // 2 - modes
    count = rows // sub
    halo = halo_ref[...]
    key = featurize(key_ref[...], halo[2:4], taps_ref[1])
    value = featurize(value_ref[...], halo[4:6], taps_ref[2])
    kv = (key * value).astype(bf16)
    kv_ref[...] = kv
    same = own_groups(sub)
    fade = jnp.exp(-rate_ref[...] * float(sub))
    for b in range(width // LANES):
        cols = slice(b * LANES, (b + 1) * LANES)
        total = jnp.zeros((modes, LANES), f32)
        for first in range(0, count, 2):
            right = []
            for s in (first, first + 1):
                piece = kv[s * sub : (s + 1) * sub, cols]
                spread = jnp.concatenate([piece] * (LANES // GROUP), axis=0)
                right.append(jnp.where(same, spread, jnp.zeros_like(spread)))
            out = dot(left_ref[b], jnp.concatenate(right, axis=1))
            for s in (first, first + 1):
                part = out[:, (s - first) * LANES : (s - first + 1) * LANES]
                inner_ref[s * sub : (s + 1) * sub, cols] = part[:sub] + part[sub : 2 * sub]
                before_ref[s * modes : (s + 1) * modes, cols] = total
                total = total * fade[:, cols] + (
                    part[2 * sub : 2 * sub + modes] + part[2 * sub + modes :]
                )
        state_ref[:, cols] = total


def blend_kernel(rows, step, where_ref, state_ref, other_ref, enter_ref, rate_ref, new_ref, into_ref):
    index = where_ref[0]
    upper = (index // step) % 2 == 1
    within = ((index % step) * rows).astype(f32)
    rate = rate_ref[...]
    state, other, enter = state_ref[...], other_ref[...], enter_ref[...]
    into_ref[...] = jnp.where(upper, enter + jnp.exp(-rate * within) * other, enter)
    fade = jnp.exp(-rate * float(step * rows))
    new_ref[...] = jnp.where(upper, other * fade + state, state * fade + other)


def gate_kernel(
    step, where_ref, query_ref, halo_ref, taps_ref, kv_ref, inner_ref, before_ref, enter_ref, other_ref,
    rate_ref, lag_ref, skip_ref, out_ref,
):
    rows, width = query_ref.shape
    modes = rate_ref.shape[0]
    sub = lag_ref.shape[1] // 2
    index = where_ref[0]
    upper = (index // step) % 2 == 1
    within = ((index % step) * rows).astype(f32)
    query = featurize(query_ref[...], halo_ref[0:2], taps_ref[0])
    rate = rate_ref[...]
    enter = enter_ref[...]
    enter = jnp.where(upper, enter + jnp.exp(-rate * within) * other_ref[...], enter)
    fade = jnp.exp(-rate * float(sub))
    same = own_groups(modes)
    for b in range(width // LANES):
        cols = slice(b * LANES, (b + 1) * LANES)
        far = enter[:, cols]
        for first in range(0, rows // sub, 2):
            right = []
            for s in (first, first + 1):
                total = far + before_ref[s * modes : (s + 1) * modes, cols]
                spread = jnp.concatenate([total] * (LANES // GROUP), axis=0)
                right.append(jnp.concatenate(split(jnp.where(same, spread, 0.0)), axis=0))
                far = far * fade[:, cols]
            cross = dot(lag_ref[b], jnp.concatenate(right, axis=1))
            for s in (first, first + 1):
                part = cross[:, (s - first) * LANES : (s - first + 1) * LANES]
                at = slice(s * sub, (s + 1) * sub)
                convolved = inner_ref[at, cols] + (part[:sub] + part[sub:])
                convolved = convolved.astype(bf16).astype(f32)
                kv = kv_ref[at, cols].astype(f32)
                out_ref[at, cols] = (query[at, cols] * (convolved + skip_ref[:, cols] * kv)).astype(bf16)


def prepare_kernel(which_ref, query_ref, key_ref, value_ref, weight_ref, tail_ref, piece_ref, rows_ref, sems):
    keep = FEAT - 1
    height = rows_ref.shape[1]
    width = piece_ref.shape[1]
    at = pl.multiple_of((which_ref[0] & 7) * width, width)
    copies = [pltpu.make_async_copy(weight_ref.at[:, pl.ds(at, width)], piece_ref, sems.at[3])]
    for i, ref in enumerate((query_ref, key_ref, value_ref)):
        first = ref.shape[0] - height
        copies.append(
            pltpu.make_async_copy(ref.at[pl.ds(first, height)], rows_ref.at[i], sems.at[i])
        )
    for copy in copies:
        copy.start()
    for copy in copies[1:]:
        copy.wait()
    for i in range(3):
        tail_ref[i * keep : (i + 1) * keep] = rows_ref[i].astype(f32)[height - keep :]
    tail_ref[3 * keep :] = jnp.zeros((tail_ref.shape[0] - 3 * keep, tail_ref.shape[1]), f32)
    copies[0].wait()


def prepare(query, key, value, weight):
    chans = query.shape[1]
    depth, cols = weight.shape
    which = lax.axis_index("ctx")[None].astype(jnp.int32)
    hbm = pl.BlockSpec(memory_space=pltpu.HBM)
    vmem = pl.BlockSpec(memory_space=pltpu.VMEM)
    return pl.pallas_call(
        prepare_kernel,
        in_specs=[pl.BlockSpec(memory_space=pltpu.SMEM)] + [hbm] * 4,
        out_specs=[vmem, vmem],
        out_shape=[
            jax.ShapeDtypeStruct((8, chans), f32),
            jax.ShapeDtypeStruct((depth, cols // 8), bf16),
        ],
        scratch_shapes=[pltpu.VMEM((3, 16, chans), bf16), pltpu.SemaphoreType.DMA((4,))],
        compiler_params=params(PREP << 20),
        name="prepare",
    )(which, query, key, value, weight)


def stack_kernel(one_ref, two_ref, out_ref):
    depth = one_ref.shape[0]
    out_ref[:depth] = one_ref[...]
    out_ref[depth:] = two_ref[...]


def stack_rows(one, two):
    depth, block = one.shape
    vmem = pl.BlockSpec(memory_space=pltpu.VMEM)
    return pl.pallas_call(
        stack_kernel,
        in_specs=[vmem, vmem],
        out_specs=vmem,
        out_shape=jax.ShapeDtypeStruct((2 * depth, block), bf16),
        compiler_params=params(),
        cost_estimate=COST,
        name="stack_rows",
    )(one, two)


def relay_kernel(in_ref, *refs):
    del in_ref, refs


def relay(x, *held):
    unused = pl.BlockSpec(memory_space=pl.ANY)
    return pl.pallas_call(
        relay_kernel,
        in_specs=[unused] * (1 + len(held)),
        out_specs=unused,
        out_shape=jax.ShapeDtypeStruct(x.shape, x.dtype),
        input_output_aliases={0: 0},
        compiler_params=params(),
        cost_estimate=COST,
        name="relay",
    )(x, *held)


def conv_path(query, key, value, halo, near, two, mine, rate, residues, taps, skip):
    rows, chans = query.shape
    groups, modes = rate.shape
    blocks = chans // LANES
    depth = LANES // GROUP * SUB
    count = lax.axis_size("ctx")
    here = lax.axis_index("ctx")[None].astype(jnp.int32)
    steps = chans // WIDE
    per = WIDE // LANES
    vmem = pl.BlockSpec(memory_space=pltpu.VMEM)
    smem = pl.BlockSpec(memory_space=pltpu.SMEM)
    state_shape = jax.ShapeDtypeStruct((modes, chans), f32)
    left, lag, rate_chan = pl.pallas_call(
        table_kernel,
        in_specs=[vmem, vmem],
        out_specs=[vmem] * 3,
        out_shape=[
            jax.ShapeDtypeStruct((blocks, 2 * (SUB + modes), depth), bf16),
            jax.ShapeDtypeStruct((blocks, 2 * SUB, 2 * (LANES // GROUP) * modes), bf16),
            state_shape,
        ],
        compiler_params=params(),
        cost_estimate=COST,
        name="tables",
    )(rate, residues)

    def wide(height):
        return pl.BlockSpec((height, WIDE), lambda b: (0, b))

    def stack(array):
        return pl.BlockSpec((per,) + array.shape[1:], lambda b: (b, 0, 0))

    taps_spec = pl.BlockSpec((3, FEAT, WIDE), lambda b: (0, 0, b))
    subs = rows // SUB
    unused = pl.BlockSpec(memory_space=pl.ANY)
    pieces = dict(z1=near, z2=two)
    held = [pieces[n] for n in HOLD[0]]
    kv, inner, before, state = pl.pallas_call(
        waiting(product_kernel, len(held), 6),
        grid=(steps,),
        in_specs=[wide(rows), wide(rows), wide(8), taps_spec, stack(left), wide(modes)] + [unused] * len(held),
        out_specs=[wide(rows), wide(rows), wide(subs * modes), wide(modes)],
        out_shape=[
            jax.ShapeDtypeStruct((rows, chans), bf16),
            jax.ShapeDtypeStruct((rows, chans), f32),
            jax.ShapeDtypeStruct((subs * modes, chans), f32),
            state_shape,
        ],
        compiler_params=params(),
        cost_estimate=COST,
        name="kv_and_state",
    )(key, value, halo, taps, left, rate_chan, *held)
    enter = jnp.zeros_like(state)
    pieces["k"] = state
    step = 1
    at = lambda array, name: relay(array, *[pieces[n] for n in RELAY[name]]) if RELAY[name] else array
    while True:
        if step == 1:
            near = at(near, "z1")
            pieces["a1"] = hop(near, True)
        other = lax.ppermute(state, "ctx", [(i, i ^ step) for i in range(count)])
        if 2 * step >= count:
            break
        held = [pieces[n] for n in HOLD[1 if step == 1 else 2]]
        state, enter = pl.pallas_call(
            waiting(functools.partial(blend_kernel, rows, step), len(held), 5),
            in_specs=[smem] + [vmem] * 4 + [unused] * len(held),
            out_specs=[vmem] * 2,
            out_shape=[state_shape] * 2,
            compiler_params=params(),
            cost_estimate=COST,
            name="blend_states",
        )(here, state, other, enter, rate_chan, *held)
        if step == 1:
            pieces["s1"] = state
            three = lax.ppermute(at(mine, "mine"), "fsdp", [(i, i ^ 3) for i in range(4)])
            pieces["z3"] = three
        if step == 2:
            pieces["s2"] = state
            two = at(two, "z2")
            pieces["a2"] = hop(two, True)
            pieces["b"] = hop(stack_rows(near, two), False)
            pieces["c"] = hop(stack_rows(pieces["a1"], pieces["a2"]), False)
        step *= 2
    pieces["y"] = other
    three = at(three, "z3")
    pieces["a3"], pieces["b3"] = hop(three, True), hop(three, False)
    pieces["c3"] = hop(at(pieces["a3"], "a3"), False)
    held = [pieces[n] for n in HOLD[3]]
    slots = [
        [near, pieces["a1"], two, pieces["a2"], pieces["b"], pieces["c"]],
        [three, pieces["a3"], pieces["b3"], pieces["c3"]],
    ]
    gated = pl.pallas_call(
        waiting(functools.partial(gate_kernel, step), len(held), 12),
        grid=(steps,),
        in_specs=[
            smem,
            wide(rows),
            wide(8),
            taps_spec,
            wide(rows),
            wide(rows),
            wide(subs * modes),
            wide(modes),
            wide(modes),
            wide(modes),
            stack(lag),
            wide(1),
        ]
        + [unused] * len(held),
        out_specs=wide(rows),
        out_shape=jax.ShapeDtypeStruct((rows, chans), bf16),
        compiler_params=params(),
        cost_estimate=COST,
        name="gate",
    )(here, query, halo, taps, kv, inner, before, enter, other, rate_chan, lag, skip[None], *held)
    return gated, slots


def hop(x, first):
    count = lax.axis_size("ctx")
    even, odd = (2, 4) if first else (4, 2)
    return lax.ppermute(x, "ctx", [(i, i ^ (odd if i % 2 else even)) for i in range(count)])


def block_order(index):
    core = index & 1
    block = index & 7
    return [block, block ^ (2 + 2 * core), block ^ (4 - 2 * core), block ^ 6]


def both_rows(mine_ref, other_ref, part, depth):
    at = pl.ds(pl.multiple_of(part * depth, depth), depth)
    return jnp.concatenate([mine_ref[:, at], other_ref[:, at]], axis=0)


def near_kernel(index_ref, place_ref, mine_ref, other_ref, weight_ref, *refs):
    index, place = index_ref[0], place_ref[0]
    near_ref, near_one, two_ref, two_one, side, corner, acc_ref = refs
    depth, block = near_ref.shape
    own, left_one, left_two = [both_rows(mine_ref, other_ref, place ^ n, depth) for n in (0, 1, 2)]
    left = jnp.concatenate([left_one, left_two], axis=1)
    for r, at in enumerate(block_order(index)):
        total = dot(own, weight_ref[:, pl.ds(pl.multiple_of(at * block, block), block)])
        if r < 2:
            one, two = ((near_ref, two_ref), (near_one, two_one))[r]
            total = total + dot(left_one, one[...]) + dot(left_two, two[...])
        else:
            total = total + dot(left, (side, corner)[r - 2][...])
        acc_ref[:, r * block : (r + 1) * block] = total


def far_kernel(index_ref, place_ref, mine_ref, other_ref, *refs):
    index, place = index_ref[0], place_ref[0]
    three, acc_ref, own_ref, out_ref = refs[:4], refs[4], refs[5], refs[6]
    depth, block = three[0].shape
    rows = mine_ref.shape[0]
    left = both_rows(mine_ref, other_ref, place ^ 3, depth)
    for r, at in enumerate(block_order(index)):
        total = acc_ref[:, r * block : (r + 1) * block] + dot(left, three[r][...])
        total = total.astype(bf16)
        cols = pl.ds(pl.multiple_of((at >> 1) * block, block), block)
        own_ref[:, cols] = total[:rows]
        out_ref[:, cols] = total[rows:]


def join_kernel(nums_ref, mine_ref, other_ref, out_ref):
    block = mine_ref.shape[1] // 4
    core = nums_ref[0] & 1
    for h in range(4):
        at = pl.multiple_of((2 * h + core) * block, block)
        out_ref[:, pl.ds(at, block)] = mine_ref[:, h * block : (h + 1) * block]
        at = pl.multiple_of((2 * h + 1 - core) * block, block)
        out_ref[:, pl.ds(at, block)] = other_ref[:, h * block : (h + 1) * block]


def project(gated, weight, slots):
    count = lax.axis_size("ctx")
    index = lax.axis_index("ctx")[None].astype(jnp.int32)
    place = lax.axis_index("fsdp")[None].astype(jnp.int32)
    rows = gated.shape[0]
    cols = weight.shape[1]
    swap = [(i, i ^ 1) for i in range(count)]
    other = lax.ppermute(gated, "ctx", swap)
    vmem = pl.BlockSpec(memory_space=pltpu.VMEM)
    smem = pl.BlockSpec(memory_space=pltpu.SMEM)

    def call(kernel, name, shapes, scalars, *args):
        return pl.pallas_call(
            kernel,
            in_specs=[smem] * len(scalars) + [vmem] * len(args),
            out_specs=[vmem] * len(shapes),
            out_shape=shapes,
            compiler_params=params(),
            cost_estimate=COST,
            name=name,
        )(*scalars, *args)

    (acc,) = call(
        near_kernel,
        "project_near",
        [jax.ShapeDtypeStruct((2 * rows, cols // 2), f32)],
        (index, place), gated, other, weight, *slots[0],
    )
    mine, theirs = call(
        far_kernel,
        "project_far",
        [jax.ShapeDtypeStruct((rows, cols // 2), bf16)] * 2,
        (index, place), gated, other, *slots[1], acc,
    )
    back = lax.ppermute(theirs, "ctx", swap)
    (out,) = call(
        join_kernel,
        "join_columns",
        [jax.ShapeDtypeStruct((rows, cols), bf16)],
        (index,), mine, back,
    )
    return out


def local(query_in, key_in, value_in, feature_taps, decay_rate, residues, skip_gain, out_weight):
    query, key, value = query_in[0], key_in[0], value_in[0]
    tails, mine = prepare(query, key, value, out_weight)
    count = lax.axis_size("ctx")
    halo = lax.ppermute(tails, "ctx", [(i, i + 1) for i in range(count - 1)])
    near = lax.ppermute(mine, "fsdp", [(i, i ^ 1) for i in range(4)])
    two = lax.ppermute(mine, "fsdp", [(i, i ^ 2) for i in range(4)])
    gated, slots = conv_path(
        query, key, value, halo, near, two, mine, decay_rate, residues, feature_taps, skip_gain
    )
    return project(gated, out_weight, slots)[None]


def solution(mesh):
    return jax.shard_map(
        local,
        mesh=mesh,
        in_specs=(
            P("fsdp", "ctx", None),
            P("fsdp", "ctx", None),
            P("fsdp", "ctx", None),
            P(),
            P(),
            P(),
            P(),
            P("fsdp", None),
        ),
        out_specs=P("fsdp", "ctx", None),
        check_vma=False,
    )
```

```python
import functools

import jax
import jax.numpy as jnp
from jax import lax
from jax.experimental import pallas as pl
from jax.experimental.pallas import tpu as pltpu
from jax.sharding import PartitionSpec as P

GROUP = 16
HOLD = [[], [], [], []]
RELAY = {'z1': [], 'a1': [], 'mine': ['z1'], 'z2': ['s1'], 'z3': ['s2'], 'a3': []}
FEAT = 3
WIDE = 512
LANES = 128
SUB = 32
VMEM_LIMIT = 48 << 20
PREP = 61
COST = pl.CostEstimate(flops=0, bytes_accessed=0, transcendentals=0)

bf16 = jnp.bfloat16
f32 = jnp.float32


def waiting(kernel, count, first):
    def body(*refs):
        kernel(*refs[:first], *refs[first + count :])

    return body


def params(limit=VMEM_LIMIT):
    return pltpu.CompilerParams(vmem_limit_bytes=limit)


def split(x):
    high = x.astype(bf16)
    return high, (x - high.astype(f32)).astype(bf16)


def iota(shape, dim):
    return lax.broadcasted_iota(jnp.int32, shape, dim)


def one_less_exp(x):
    small = jnp.minimum(x, 0.5)
    series = jnp.ones_like(x)
    for n in range(9, 1, -1):
        series = 1.0 - small * (1.0 / n) * series
    return jnp.where(x < 0.5, small * series, 1.0 - jnp.exp(-x))


def dot(a, b):
    return jnp.dot(a, b, preferred_element_type=f32)


def featurize(rows, tail, taps):
    values = rows.astype(f32)
    at = iota(values.shape, 0)
    one = jnp.where(at == 0, tail[1:2], pltpu.roll(values, 1, 0))
    two = jnp.where(at == 0, tail[0:1], jnp.where(at == 1, tail[1:2], pltpu.roll(values, 2, 0)))
    return taps[0:1] * values + taps[1:2] * one + taps[2:3] * two


def table_kernel(rate_ref, residue_ref, left_ref, lag_ref, rate_chan_ref):
    rate = rate_ref[...]
    groups, modes = rate.shape
    scale = residue_ref[...] * jnp.sqrt(one_less_exp(2.0 * rate))
    blocks, _, depth = left_ref.shape
    sub = left_ref.shape[1] // 2 - modes
    each = groups // blocks

    def expand(table, width, count):
        pick = iota((groups, count), 0) == iota((groups, count), 1) // width
        pick = pick.astype(bf16)
        high = table.astype(bf16)
        rest = table - high.astype(f32)
        middle, low = split(rest)
        return dot(high, pick) + (dot(middle, pick) + dot(low, pick))

    rate_turned, scale_turned = rate.T, scale.T
    rate_chan_ref[...] = expand(rate_turned, GROUP, groups * GROUP)
    rate_wide = expand(rate_turned, sub, groups * sub)
    scale_wide = expand(scale_turned, sub, groups * sub)
    place = iota((modes, groups * sub), 1) % sub
    back = jnp.where(place == 0, 0, sub - place).astype(f32)
    taps = jnp.sum(scale_wide * jnp.exp(-rate_wide * back), axis=0, keepdims=True)
    ends = scale_wide * jnp.exp(-rate_wide * (sub - 1 - place).astype(f32))
    end_high, end_low = split(ends)
    causal = iota((sub, LANES), 0) >= iota((sub, LANES), 1) % sub
    start = iota((1, LANES), 1) % sub == 0
    mode_pick = iota((modes, each * modes), 0) == iota((modes, each * modes), 1) % modes
    group_at = iota((groups, each * modes), 1) // modes
    ahead = (iota((sub, each * modes), 0) + 1).astype(f32)
    for b in range(blocks):
        for part in range(depth // LANES):
            at = b * depth + part * LANES
            row = taps[:, at : at + LANES]
            row = jnp.where(start, row, pltpu.roll(row, LANES - sub, 1))
            band = pltpu.roll(jnp.broadcast_to(row, (sub, LANES)), 0, 1, stride=1, stride_axis=0)
            high, low = split(jnp.where(causal, band, 0.0))
            to = slice(part * LANES, (part + 1) * LANES)
            left_ref[b, :sub, to] = high
            left_ref[b, sub : 2 * sub, to] = low
        cols = slice(b * depth, (b + 1) * depth)
        left_ref[b, 2 * sub : 2 * sub + modes] = end_high[:, cols]
        left_ref[b, 2 * sub + modes :] = end_low[:, cols]
        spread = jnp.dot(
            (iota((groups, each * modes), 0) == b * each + group_at).astype(f32).T,
            rate,
            precision=lax.Precision.HIGHEST,
            preferred_element_type=f32,
        )
        rate_lane = jnp.sum(jnp.where(mode_pick, spread.T, 0.0), axis=0, keepdims=True)
        high, low = split(jnp.exp(-rate_lane * ahead))
        lag_ref[b, :sub] = jnp.concatenate([high, high], axis=1)
        lag_ref[b, sub:] = jnp.concatenate([low, jnp.zeros_like(low)], axis=1)


def own_groups(rows_each):
    rows = LANES // GROUP * rows_each
    return iota((rows, LANES), 0) // rows_each == iota((rows, LANES), 1) // GROUP


def product_kernel(
    key_ref, value_ref, halo_ref, taps_ref, left_ref, rate_ref, kv_ref, inner_ref, before_ref, state_ref
):
    rows, width = key_ref.shape
    modes = rate_ref.shape[0]
    sub = left_ref.shape[1] // 2 - modes
    count = rows // sub
    halo = halo_ref[...]
    key = featurize(key_ref[...], halo[2:4], taps_ref[1])
    value = featurize(value_ref[...], halo[4:6], taps_ref[2])
    kv = (key * value).astype(bf16)
    kv_ref[...] = kv
    same = own_groups(sub)
    fade = jnp.exp(-rate_ref[...] * float(sub))
    for b in range(width // LANES):
        cols = slice(b * LANES, (b + 1) * LANES)
        total = jnp.zeros((modes, LANES), f32)
        for first in range(0, count, 2):
            right = []
            for s in (first, first + 1):
                piece = kv[s * sub : (s + 1) * sub, cols]
                spread = jnp.concatenate([piece] * (LANES // GROUP), axis=0)
                right.append(jnp.where(same, spread, jnp.zeros_like(spread)))
            out = dot(left_ref[b], jnp.concatenate(right, axis=1))
            for s in (first, first + 1):
                part = out[:, (s - first) * LANES : (s - first + 1) * LANES]
                inner_ref[s * sub : (s + 1) * sub, cols] = part[:sub] + part[sub : 2 * sub]
                before_ref[s * modes : (s + 1) * modes, cols] = total
                total = total * fade[:, cols] + (
                    part[2 * sub : 2 * sub + modes] + part[2 * sub + modes :]
                )
        state_ref[:, cols] = total


def blend_kernel(rows, step, where_ref, state_ref, other_ref, enter_ref, rate_ref, new_ref, into_ref):
    index = where_ref[0]
    upper = (index // step) % 2 == 1
    within = ((index % step) * rows).astype(f32)
    rate = rate_ref[...]
    state, other, enter = state_ref[...], other_ref[...], enter_ref[...]
    into_ref[...] = jnp.where(upper, enter + jnp.exp(-rate * within) * other, enter)
    fade = jnp.exp(-rate * float(step * rows))
    new_ref[...] = jnp.where(upper, other * fade + state, state * fade + other)


def gate_kernel(
    step, where_ref, query_ref, halo_ref, taps_ref, kv_ref, inner_ref, before_ref, enter_ref, other_ref,
    rate_ref, lag_ref, skip_ref, out_ref,
):
    rows, width = query_ref.shape
    modes = rate_ref.shape[0]
    sub = lag_ref.shape[1] // 2
    index = where_ref[0]
    upper = (index // step) % 2 == 1
    within = ((index % step) * rows).astype(f32)
    query = featurize(query_ref[...], halo_ref[0:2], taps_ref[0])
    rate = rate_ref[...]
    enter = enter_ref[...]
    enter = jnp.where(upper, enter + jnp.exp(-rate * within) * other_ref[...], enter)
    fade = jnp.exp(-rate * float(sub))
    same = own_groups(modes)
    for b in range(width // LANES):
        cols = slice(b * LANES, (b + 1) * LANES)
        far = enter[:, cols]
        for first in range(0, rows // sub, 2):
            right = []
            for s in (first, first + 1):
                total = far + before_ref[s * modes : (s + 1) * modes, cols]
                spread = jnp.concatenate([total] * (LANES // GROUP), axis=0)
                right.append(jnp.concatenate(split(jnp.where(same, spread, 0.0)), axis=0))
                far = far * fade[:, cols]
            cross = dot(lag_ref[b], jnp.concatenate(right, axis=1))
            for s in (first, first + 1):
                part = cross[:, (s - first) * LANES : (s - first + 1) * LANES]
                at = slice(s * sub, (s + 1) * sub)
                convolved = inner_ref[at, cols] + (part[:sub] + part[sub:])
                convolved = convolved.astype(bf16).astype(f32)
                kv = kv_ref[at, cols].astype(f32)
                out_ref[at, cols] = (query[at, cols] * (convolved + skip_ref[:, cols] * kv)).astype(bf16)


def prepare_kernel(which_ref, query_ref, key_ref, value_ref, weight_ref, tail_ref, piece_ref, rows_ref, sems):
    keep = FEAT - 1
    height = rows_ref.shape[1]
    width = piece_ref.shape[1]
    at = pl.multiple_of((which_ref[0] & 7) * width, width)
    copies = [pltpu.make_async_copy(weight_ref.at[:, pl.ds(at, width)], piece_ref, sems.at[3])]
    for i, ref in enumerate((query_ref, key_ref, value_ref)):
        first = ref.shape[0] - height
        copies.append(
            pltpu.make_async_copy(ref.at[pl.ds(first, height)], rows_ref.at[i], sems.at[i])
        )
    for copy in copies:
        copy.start()
    for copy in copies[1:]:
        copy.wait()
    for i in range(3):
        tail_ref[i * keep : (i + 1) * keep] = rows_ref[i].astype(f32)[height - keep :]
    tail_ref[3 * keep :] = jnp.zeros((tail_ref.shape[0] - 3 * keep, tail_ref.shape[1]), f32)
    copies[0].wait()


def prepare(query, key, value, weight):
    chans = query.shape[1]
    depth, cols = weight.shape
    which = lax.axis_index("ctx")[None].astype(jnp.int32)
    hbm = pl.BlockSpec(memory_space=pltpu.HBM)
    vmem = pl.BlockSpec(memory_space=pltpu.VMEM)
    return pl.pallas_call(
        prepare_kernel,
        in_specs=[pl.BlockSpec(memory_space=pltpu.SMEM)] + [hbm] * 4,
        out_specs=[vmem, vmem],
        out_shape=[
            jax.ShapeDtypeStruct((8, chans), f32),
            jax.ShapeDtypeStruct((depth, cols // 8), bf16),
        ],
        scratch_shapes=[pltpu.VMEM((3, 16, chans), bf16), pltpu.SemaphoreType.DMA((4,))],
        compiler_params=params(PREP << 20),
        name="prepare",
    )(which, query, key, value, weight)


def stack_kernel(one_ref, two_ref, out_ref):
    depth = one_ref.shape[0]
    out_ref[:depth] = one_ref[...]
    out_ref[depth:] = two_ref[...]


def stack_rows(one, two):
    depth, block = one.shape
    vmem = pl.BlockSpec(memory_space=pltpu.VMEM)
    return pl.pallas_call(
        stack_kernel,
        in_specs=[vmem, vmem],
        out_specs=vmem,
        out_shape=jax.ShapeDtypeStruct((2 * depth, block), bf16),
        compiler_params=params(),
        cost_estimate=COST,
        name="stack_rows",
    )(one, two)


def relay_kernel(in_ref, *refs):
    del in_ref, refs


def relay(x, *held):
    unused = pl.BlockSpec(memory_space=pl.ANY)
    return pl.pallas_call(
        relay_kernel,
        in_specs=[unused] * (1 + len(held)),
        out_specs=unused,
        out_shape=jax.ShapeDtypeStruct(x.shape, x.dtype),
        input_output_aliases={0: 0},
        compiler_params=params(),
        cost_estimate=COST,
        name="relay",
    )(x, *held)


def conv_path(query, key, value, halo, near, two, mine, rate, residues, taps, skip):
    rows, chans = query.shape
    groups, modes = rate.shape
    blocks = chans // LANES
    depth = LANES // GROUP * SUB
    count = lax.axis_size("ctx")
    here = lax.axis_index("ctx")[None].astype(jnp.int32)
    steps = chans // WIDE
    per = WIDE // LANES
    vmem = pl.BlockSpec(memory_space=pltpu.VMEM)
    smem = pl.BlockSpec(memory_space=pltpu.SMEM)
    state_shape = jax.ShapeDtypeStruct((modes, chans), f32)
    left, lag, rate_chan = pl.pallas_call(
        table_kernel,
        in_specs=[vmem, vmem],
        out_specs=[vmem] * 3,
        out_shape=[
            jax.ShapeDtypeStruct((blocks, 2 * (SUB + modes), depth), bf16),
            jax.ShapeDtypeStruct((blocks, 2 * SUB, 2 * (LANES // GROUP) * modes), bf16),
            state_shape,
        ],
        compiler_params=params(),
        cost_estimate=COST,
        name="tables",
    )(rate, residues)

    def wide(height):
        return pl.BlockSpec((height, WIDE), lambda b: (0, b))

    def stack(array):
        return pl.BlockSpec((per,) + array.shape[1:], lambda b: (b, 0, 0))

    taps_spec = pl.BlockSpec((3, FEAT, WIDE), lambda b: (0, 0, b))
    subs = rows // SUB
    unused = pl.BlockSpec(memory_space=pl.ANY)
    pieces = dict(z1=near, z2=two)
    held = [pieces[n] for n in HOLD[0]]
    kv, inner, before, state = pl.pallas_call(
        waiting(product_kernel, len(held), 6),
        grid=(steps,),
        in_specs=[wide(rows), wide(rows), wide(8), taps_spec, stack(left), wide(modes)] + [unused] * len(held),
        out_specs=[wide(rows), wide(rows), wide(subs * modes), wide(modes)],
        out_shape=[
            jax.ShapeDtypeStruct((rows, chans), bf16),
            jax.ShapeDtypeStruct((rows, chans), f32),
            jax.ShapeDtypeStruct((subs * modes, chans), f32),
            state_shape,
        ],
        compiler_params=params(),
        cost_estimate=COST,
        name="kv_and_state",
    )(key, value, halo, taps, left, rate_chan, *held)
    enter = jnp.zeros_like(state)
    pieces["k"] = state
    step = 1
    at = lambda array, name: relay(array, *[pieces[n] for n in RELAY[name]]) if RELAY[name] else array
    while True:
        if step == 1:
            near = at(near, "z1")
            pieces["a1"] = hop(near, True)
        other = lax.ppermute(state, "ctx", [(i, i ^ step) for i in range(count)])
        if 2 * step >= count:
            break
        held = [pieces[n] for n in HOLD[1 if step == 1 else 2]]
        state, enter = pl.pallas_call(
            waiting(functools.partial(blend_kernel, rows, step), len(held), 5),
            in_specs=[smem] + [vmem] * 4 + [unused] * len(held),
            out_specs=[vmem] * 2,
            out_shape=[state_shape] * 2,
            compiler_params=params(),
            cost_estimate=COST,
            name="blend_states",
        )(here, state, other, enter, rate_chan, *held)
        if step == 1:
            pieces["s1"] = state
            three = lax.ppermute(at(mine, "mine"), "fsdp", [(i, i ^ 3) for i in range(4)])
            pieces["z3"] = three
        if step == 2:
            pieces["s2"] = state
            two = at(two, "z2")
            pieces["a2"] = hop(two, True)
            pieces["b"] = hop(stack_rows(near, two), False)
            pieces["c"] = hop(stack_rows(pieces["a1"], pieces["a2"]), False)
        step *= 2
    pieces["y"] = other
    three = at(three, "z3")
    pieces["a3"], pieces["b3"] = hop(three, True), hop(three, False)
    pieces["c3"] = hop(at(pieces["a3"], "a3"), False)
    held = [pieces[n] for n in HOLD[3]]
    slots = [
        [near, pieces["a1"], two, pieces["a2"], pieces["b"], pieces["c"]],
        [three, pieces["a3"], pieces["b3"], pieces["c3"]],
    ]
    gated = pl.pallas_call(
        waiting(functools.partial(gate_kernel, step), len(held), 12),
        grid=(steps,),
        in_specs=[
            smem,
            wide(rows),
            wide(8),
            taps_spec,
            wide(rows),
            wide(rows),
            wide(subs * modes),
            wide(modes),
            wide(modes),
            wide(modes),
            stack(lag),
            wide(1),
        ]
        + [unused] * len(held),
        out_specs=wide(rows),
        out_shape=jax.ShapeDtypeStruct((rows, chans), bf16),
        compiler_params=params(),
        cost_estimate=COST,
        name="gate",
    )(here, query, halo, taps, kv, inner, before, enter, other, rate_chan, lag, skip[None], *held)
    return gated, slots


def hop(x, first):
    count = lax.axis_size("ctx")
    even, odd = (2, 4) if first else (4, 2)
    return lax.ppermute(x, "ctx", [(i, i ^ (odd if i % 2 else even)) for i in range(count)])


def block_order(index):
    core = index & 1
    block = index & 7
    return [block, block ^ (2 + 2 * core), block ^ (4 - 2 * core), block ^ 6]


def both_rows(mine_ref, other_ref, part, depth):
    at = pl.ds(pl.multiple_of(part * depth, depth), depth)
    return jnp.concatenate([mine_ref[:, at], other_ref[:, at]], axis=0)


def near_kernel(index_ref, place_ref, mine_ref, other_ref, weight_ref, *refs):
    index, place = index_ref[0], place_ref[0]
    near_ref, near_one, two_ref, two_one, side, corner, acc_ref = refs
    depth, block = near_ref.shape
    own, left_one, left_two = [both_rows(mine_ref, other_ref, place ^ n, depth) for n in (0, 1, 2)]
    left = jnp.concatenate([left_one, left_two], axis=1)
    for r, at in enumerate(block_order(index)):
        total = dot(own, weight_ref[:, pl.ds(pl.multiple_of(at * block, block), block)])
        if r < 2:
            one, two = ((near_ref, two_ref), (near_one, two_one))[r]
            total = total + dot(left_one, one[...]) + dot(left_two, two[...])
        else:
            total = total + dot(left, (side, corner)[r - 2][...])
        acc_ref[:, r * block : (r + 1) * block] = total


def far_kernel(first, index_ref, place_ref, gated_ref, *refs):
    index, place = index_ref[0], place_ref[0]
    three, acc_ref, out_ref = refs[:4], refs[4], refs[5]
    depth, block = three[0].shape
    rows = gated_ref.shape[0]
    left = gated_ref[:, pl.ds(pl.multiple_of((place ^ 3) * depth, depth), depth)]
    for r, at in enumerate(block_order(index)):
        total = acc_ref[first : first + rows, r * block : (r + 1) * block] + dot(left, three[r][...])
        cols = pl.ds(pl.multiple_of((at >> 1) * block, block), block)
        out_ref[:, cols] = total.astype(bf16)


def join_kernel(nums_ref, mine_ref, other_ref, out_ref):
    block = mine_ref.shape[1] // 4
    core = nums_ref[0] & 1
    for h in range(4):
        at = pl.multiple_of((2 * h + core) * block, block)
        out_ref[:, pl.ds(at, block)] = mine_ref[:, h * block : (h + 1) * block]
        at = pl.multiple_of((2 * h + 1 - core) * block, block)
        out_ref[:, pl.ds(at, block)] = other_ref[:, h * block : (h + 1) * block]


def project(gated, weight, slots):
    count = lax.axis_size("ctx")
    index = lax.axis_index("ctx")[None].astype(jnp.int32)
    place = lax.axis_index("fsdp")[None].astype(jnp.int32)
    rows = gated.shape[0]
    cols = weight.shape[1]
    swap = [(i, i ^ 1) for i in range(count)]
    other = lax.ppermute(gated, "ctx", swap)
    vmem = pl.BlockSpec(memory_space=pltpu.VMEM)
    smem = pl.BlockSpec(memory_space=pltpu.SMEM)

    def call(kernel, name, shapes, scalars, *args):
        return pl.pallas_call(
            kernel,
            in_specs=[smem] * len(scalars) + [vmem] * len(args),
            out_specs=[vmem] * len(shapes),
            out_shape=shapes,
            compiler_params=params(),
            cost_estimate=COST,
            name=name,
        )(*scalars, *args)

    (acc,) = call(
        near_kernel,
        "project_near",
        [jax.ShapeDtypeStruct((2 * rows, cols // 2), f32)],
        (index, place), gated, other, weight, *slots[0],
    )
    half = [jax.ShapeDtypeStruct((rows, cols // 2), bf16)]
    (theirs,) = call(
        functools.partial(far_kernel, rows), "project_theirs", half, (index, place), other, *slots[1], acc
    )
    back = lax.ppermute(theirs, "ctx", swap)
    (mine,) = call(
        functools.partial(far_kernel, 0), "project_mine", half, (index, place), gated, *slots[1], acc
    )
    (out,) = call(
        join_kernel,
        "join_columns",
        [jax.ShapeDtypeStruct((rows, cols), bf16)],
        (index,), mine, back,
    )
    return out


def local(query_in, key_in, value_in, feature_taps, decay_rate, residues, skip_gain, out_weight):
    query, key, value = query_in[0], key_in[0], value_in[0]
    tails, mine = prepare(query, key, value, out_weight)
    count = lax.axis_size("ctx")
    halo = lax.ppermute(tails, "ctx", [(i, i + 1) for i in range(count - 1)])
    near = lax.ppermute(mine, "fsdp", [(i, i ^ 1) for i in range(4)])
    two = lax.ppermute(mine, "fsdp", [(i, i ^ 2) for i in range(4)])
    gated, slots = conv_path(
        query, key, value, halo, near, two, mine, decay_rate, residues, feature_taps, skip_gain
    )
    return project(gated, out_weight, slots)[None]


def solution(mesh):
    return jax.shard_map(
        local,
        mesh=mesh,
        in_specs=(
            P("fsdp", "ctx", None),
            P("fsdp", "ctx", None),
            P("fsdp", "ctx", None),
            P(),
            P(),
            P(),
            P(),
            P("fsdp", None),
        ),
        out_specs=P("fsdp", "ctx", None),
        check_vma=False,
    )
```

```python
import functools

import jax
import jax.numpy as jnp
from jax import lax
from jax.experimental import pallas as pl
from jax.experimental.pallas import tpu as pltpu
from jax.sharding import PartitionSpec as P

GROUP = 16
HOLD = [[], [], [], []]
RELAY = {'z1': [], 'a1': [], 'mine': ['z1'], 'z2': ['s1'], 'z3': ['s2'], 'a3': []}
FEAT = 3
WIDE = 1024
LANES = 128
SUB = 32
VMEM_LIMIT = 48 << 20
PREP = 61
COST = pl.CostEstimate(flops=0, bytes_accessed=0, transcendentals=0)

bf16 = jnp.bfloat16
f32 = jnp.float32


def waiting(kernel, count, first):
    def body(*refs):
        kernel(*refs[:first], *refs[first + count :])

    return body


def params(limit=VMEM_LIMIT):
    return pltpu.CompilerParams(vmem_limit_bytes=limit)


def split(x):
    high = x.astype(bf16)
    return high, (x - high.astype(f32)).astype(bf16)


def iota(shape, dim):
    return lax.broadcasted_iota(jnp.int32, shape, dim)


def one_less_exp(x):
    small = jnp.minimum(x, 0.5)
    series = jnp.ones_like(x)
    for n in range(9, 1, -1):
        series = 1.0 - small * (1.0 / n) * series
    return jnp.where(x < 0.5, small * series, 1.0 - jnp.exp(-x))


def dot(a, b):
    return jnp.dot(a, b, preferred_element_type=f32)


def featurize(rows, tail, taps):
    values = rows.astype(f32)
    at = iota(values.shape, 0)
    one = jnp.where(at == 0, tail[1:2], pltpu.roll(values, 1, 0))
    two = jnp.where(at == 0, tail[0:1], jnp.where(at == 1, tail[1:2], pltpu.roll(values, 2, 0)))
    return taps[0:1] * values + taps[1:2] * one + taps[2:3] * two


def table_kernel(rate_ref, residue_ref, left_ref, lag_ref, rate_chan_ref):
    rate = rate_ref[...]
    groups, modes = rate.shape
    scale = residue_ref[...] * jnp.sqrt(one_less_exp(2.0 * rate))
    blocks, _, depth = left_ref.shape
    sub = left_ref.shape[1] // 2 - modes
    each = groups // blocks

    def expand(table, width, count):
        pick = iota((groups, count), 0) == iota((groups, count), 1) // width
        pick = pick.astype(bf16)
        high = table.astype(bf16)
        rest = table - high.astype(f32)
        middle, low = split(rest)
        return dot(high, pick) + (dot(middle, pick) + dot(low, pick))

    rate_turned, scale_turned = rate.T, scale.T
    rate_chan_ref[...] = expand(rate_turned, GROUP, groups * GROUP)
    rate_wide = expand(rate_turned, sub, groups * sub)
    scale_wide = expand(scale_turned, sub, groups * sub)
    place = iota((modes, groups * sub), 1) % sub
    back = jnp.where(place == 0, 0, sub - place).astype(f32)
    taps = jnp.sum(scale_wide * jnp.exp(-rate_wide * back), axis=0, keepdims=True)
    ends = scale_wide * jnp.exp(-rate_wide * (sub - 1 - place).astype(f32))
    end_high, end_low = split(ends)
    causal = iota((sub, LANES), 0) >= iota((sub, LANES), 1) % sub
    start = iota((1, LANES), 1) % sub == 0
    spread = rate_chan_ref[...] if modes == GROUP else expand(rate_turned, modes, groups * modes)
    mode_pick = iota((modes, groups * modes), 0) == iota((modes, groups * modes), 1) % modes
    rate_lane = jnp.sum(jnp.where(mode_pick, spread, 0.0), axis=0, keepdims=True)
    ahead = (iota((sub, each * modes), 0) + 1).astype(f32)
    for b in range(blocks):
        for part in range(depth // LANES):
            at = b * depth + part * LANES
            row = taps[:, at : at + LANES]
            row = jnp.where(start, row, pltpu.roll(row, LANES - sub, 1))
            band = pltpu.roll(jnp.broadcast_to(row, (sub, LANES)), 0, 1, stride=1, stride_axis=0)
            high, low = split(jnp.where(causal, band, 0.0))
            to = slice(part * LANES, (part + 1) * LANES)
            left_ref[b, :sub, to] = high
            left_ref[b, sub : 2 * sub, to] = low
        cols = slice(b * depth, (b + 1) * depth)
        left_ref[b, 2 * sub : 2 * sub + modes] = end_high[:, cols]
        left_ref[b, 2 * sub + modes :] = end_low[:, cols]
        lane = rate_lane[:, b * each * modes : (b + 1) * each * modes]
        high, low = split(jnp.exp(-lane * ahead))
        lag_ref[b, :sub] = jnp.concatenate([high, high], axis=1)
        lag_ref[b, sub:] = jnp.concatenate([low, jnp.zeros_like(low)], axis=1)


def own_groups(rows_each):
    rows = LANES // GROUP * rows_each
    return iota((rows, LANES), 0) // rows_each == iota((rows, LANES), 1) // GROUP


def product_kernel(
    key_ref, value_ref, halo_ref, taps_ref, left_ref, rate_ref, kv_ref, inner_ref, before_ref, state_ref
):
    rows, width = key_ref.shape
    modes = rate_ref.shape[0]
    sub = left_ref.shape[1] // 2 - modes
    count = rows // sub
    halo = halo_ref[...]
    key = featurize(key_ref[...], halo[2:4], taps_ref[1])
    value = featurize(value_ref[...], halo[4:6], taps_ref[2])
    kv = (key * value).astype(bf16)
    kv_ref[...] = kv
    same = own_groups(sub)
    fade = jnp.exp(-rate_ref[...] * float(sub))
    for b in range(width // LANES):
        cols = slice(b * LANES, (b + 1) * LANES)
        total = jnp.zeros((modes, LANES), f32)
        for first in range(0, count, 2):
            right = []
            for s in (first, first + 1):
                piece = kv[s * sub : (s + 1) * sub, cols]
                spread = jnp.concatenate([piece] * (LANES // GROUP), axis=0)
                right.append(jnp.where(same, spread, jnp.zeros_like(spread)))
            out = dot(left_ref[b], jnp.concatenate(right, axis=1))
            for s in (first, first + 1):
                part = out[:, (s - first) * LANES : (s - first + 1) * LANES]
                inner_ref[s * sub : (s + 1) * sub, cols] = part[:sub] + part[sub : 2 * sub]
                before_ref[s * modes : (s + 1) * modes, cols] = total
                total = total * fade[:, cols] + (
                    part[2 * sub : 2 * sub + modes] + part[2 * sub + modes :]
                )
        state_ref[:, cols] = total


def blend_kernel(rows, step, where_ref, state_ref, other_ref, enter_ref, rate_ref, new_ref, into_ref):
    index = where_ref[0]
    upper = (index // step) % 2 == 1
    within = ((index % step) * rows).astype(f32)
    rate = rate_ref[...]
    state, other, enter = state_ref[...], other_ref[...], enter_ref[...]
    into_ref[...] = jnp.where(upper, enter + jnp.exp(-rate * within) * other, enter)
    fade = jnp.exp(-rate * float(step * rows))
    new_ref[...] = jnp.where(upper, other * fade + state, state * fade + other)


def gate_kernel(
    step, where_ref, query_ref, halo_ref, taps_ref, kv_ref, inner_ref, before_ref, enter_ref, other_ref,
    rate_ref, lag_ref, skip_ref, out_ref,
):
    rows, width = query_ref.shape
    modes = rate_ref.shape[0]
    sub = lag_ref.shape[1] // 2
    index = where_ref[0]
    upper = (index // step) % 2 == 1
    within = ((index % step) * rows).astype(f32)
    query = featurize(query_ref[...], halo_ref[0:2], taps_ref[0])
    rate = rate_ref[...]
    enter = enter_ref[...]
    enter = jnp.where(upper, enter + jnp.exp(-rate * within) * other_ref[...], enter)
    fade = jnp.exp(-rate * float(sub))
    same = own_groups(modes)
    for b in range(width // LANES):
        cols = slice(b * LANES, (b + 1) * LANES)
        far = enter[:, cols]
        for first in range(0, rows // sub, 2):
            right = []
            for s in (first, first + 1):
                total = far + before_ref[s * modes : (s + 1) * modes, cols]
                spread = jnp.concatenate([total] * (LANES // GROUP), axis=0)
                right.append(jnp.concatenate(split(jnp.where(same, spread, 0.0)), axis=0))
                far = far * fade[:, cols]
            cross = dot(lag_ref[b], jnp.concatenate(right, axis=1))
            for s in (first, first + 1):
                part = cross[:, (s - first) * LANES : (s - first + 1) * LANES]
                at = slice(s * sub, (s + 1) * sub)
                convolved = inner_ref[at, cols] + (part[:sub] + part[sub:])
                convolved = convolved.astype(bf16).astype(f32)
                kv = kv_ref[at, cols].astype(f32)
                out_ref[at, cols] = (query[at, cols] * (convolved + skip_ref[:, cols] * kv)).astype(bf16)


def prepare_kernel(which_ref, query_ref, key_ref, value_ref, weight_ref, tail_ref, piece_ref, rows_ref, sems):
    keep = FEAT - 1
    height = rows_ref.shape[1]
    width = piece_ref.shape[1]
    at = pl.multiple_of((which_ref[0] & 7) * width, width)
    copies = [pltpu.make_async_copy(weight_ref.at[:, pl.ds(at, width)], piece_ref, sems.at[3])]
    for i, ref in enumerate((query_ref, key_ref, value_ref)):
        first = ref.shape[0] - height
        copies.append(
            pltpu.make_async_copy(ref.at[pl.ds(first, height)], rows_ref.at[i], sems.at[i])
        )
    for copy in copies:
        copy.start()
    for copy in copies[1:]:
        copy.wait()
    for i in range(3):
        tail_ref[i * keep : (i + 1) * keep] = rows_ref[i].astype(f32)[height - keep :]
    tail_ref[3 * keep :] = jnp.zeros((tail_ref.shape[0] - 3 * keep, tail_ref.shape[1]), f32)
    copies[0].wait()


def prepare(query, key, value, weight):
    chans = query.shape[1]
    depth, cols = weight.shape
    which = lax.axis_index("ctx")[None].astype(jnp.int32)
    hbm = pl.BlockSpec(memory_space=pltpu.HBM)
    vmem = pl.BlockSpec(memory_space=pltpu.VMEM)
    return pl.pallas_call(
        prepare_kernel,
        in_specs=[pl.BlockSpec(memory_space=pltpu.SMEM)] + [hbm] * 4,
        out_specs=[vmem, vmem],
        out_shape=[
            jax.ShapeDtypeStruct((8, chans), f32),
            jax.ShapeDtypeStruct((depth, cols // 8), bf16),
        ],
        scratch_shapes=[pltpu.VMEM((3, 16, chans), bf16), pltpu.SemaphoreType.DMA((4,))],
        compiler_params=params(PREP << 20),
        name="prepare",
    )(which, query, key, value, weight)


def stack_kernel(one_ref, two_ref, out_ref):
    depth = one_ref.shape[0]
    out_ref[:depth] = one_ref[...]
    out_ref[depth:] = two_ref[...]


def stack_rows(one, two):
    depth, block = one.shape
    vmem = pl.BlockSpec(memory_space=pltpu.VMEM)
    return pl.pallas_call(
        stack_kernel,
        in_specs=[vmem, vmem],
        out_specs=vmem,
        out_shape=jax.ShapeDtypeStruct((2 * depth, block), bf16),
        compiler_params=params(),
        cost_estimate=COST,
        name="stack_rows",
    )(one, two)


def relay_kernel(in_ref, *refs):
    del in_ref, refs


def relay(x, *held):
    unused = pl.BlockSpec(memory_space=pl.ANY)
    return pl.pallas_call(
        relay_kernel,
        in_specs=[unused] * (1 + len(held)),
        out_specs=unused,
        out_shape=jax.ShapeDtypeStruct(x.shape, x.dtype),
        input_output_aliases={0: 0},
        compiler_params=params(),
        cost_estimate=COST,
        name="relay",
    )(x, *held)


def conv_path(query, key, value, halo, near, two, mine, rate, residues, taps, skip):
    rows, chans = query.shape
    groups, modes = rate.shape
    blocks = chans // LANES
    depth = LANES // GROUP * SUB
    count = lax.axis_size("ctx")
    here = lax.axis_index("ctx")[None].astype(jnp.int32)
    steps = chans // WIDE
    per = WIDE // LANES
    vmem = pl.BlockSpec(memory_space=pltpu.VMEM)
    smem = pl.BlockSpec(memory_space=pltpu.SMEM)
    state_shape = jax.ShapeDtypeStruct((modes, chans), f32)
    left, lag, rate_chan = pl.pallas_call(
        table_kernel,
        in_specs=[vmem, vmem],
        out_specs=[vmem] * 3,
        out_shape=[
            jax.ShapeDtypeStruct((blocks, 2 * (SUB + modes), depth), bf16),
            jax.ShapeDtypeStruct((blocks, 2 * SUB, 2 * (LANES // GROUP) * modes), bf16),
            state_shape,
        ],
        compiler_params=params(),
        cost_estimate=COST,
        name="tables",
    )(rate, residues)

    def wide(height):
        return pl.BlockSpec((height, WIDE), lambda b: (0, b))

    def stack(array):
        return pl.BlockSpec((per,) + array.shape[1:], lambda b: (b, 0, 0))

    taps_spec = pl.BlockSpec((3, FEAT, WIDE), lambda b: (0, 0, b))
    subs = rows // SUB
    unused = pl.BlockSpec(memory_space=pl.ANY)
    pieces = dict(z1=near, z2=two)
    held = [pieces[n] for n in HOLD[0]]
    kv, inner, before, state = pl.pallas_call(
        waiting(product_kernel, len(held), 6),
        grid=(steps,),
        in_specs=[wide(rows), wide(rows), wide(8), taps_spec, stack(left), wide(modes)] + [unused] * len(held),
        out_specs=[wide(rows), wide(rows), wide(subs * modes), wide(modes)],
        out_shape=[
            jax.ShapeDtypeStruct((rows, chans), bf16),
            jax.ShapeDtypeStruct((rows, chans), f32),
            jax.ShapeDtypeStruct((subs * modes, chans), f32),
            state_shape,
        ],
        compiler_params=params(),
        cost_estimate=COST,
        name="kv_and_state",
    )(key, value, halo, taps, left, rate_chan, *held)
    enter = jnp.zeros_like(state)
    pieces["k"] = state
    step = 1
    at = lambda array, name: relay(array, *[pieces[n] for n in RELAY[name]]) if RELAY[name] else array
    while True:
        if step == 1:
            near = at(near, "z1")
            pieces["a1"] = hop(near, True)
        other = lax.ppermute(state, "ctx", [(i, i ^ step) for i in range(count)])
        if 2 * step >= count:
            break
        held = [pieces[n] for n in HOLD[1 if step == 1 else 2]]
        state, enter = pl.pallas_call(
            waiting(functools.partial(blend_kernel, rows, step), len(held), 5),
            in_specs=[smem] + [vmem] * 4 + [unused] * len(held),
            out_specs=[vmem] * 2,
            out_shape=[state_shape] * 2,
            compiler_params=params(),
            cost_estimate=COST,
            name="blend_states",
        )(here, state, other, enter, rate_chan, *held)
        if step == 1:
            pieces["s1"] = state
            three = lax.ppermute(at(mine, "mine"), "fsdp", [(i, i ^ 3) for i in range(4)])
            pieces["z3"] = three
        if step == 2:
            pieces["s2"] = state
            two = at(two, "z2")
            pieces["a2"] = hop(two, True)
            pieces["b"] = hop(stack_rows(near, two), False)
            pieces["c"] = hop(stack_rows(pieces["a1"], pieces["a2"]), False)
        step *= 2
    pieces["y"] = other
    three = at(three, "z3")
    pieces["a3"], pieces["b3"] = hop(three, True), hop(three, False)
    pieces["c3"] = hop(at(pieces["a3"], "a3"), False)
    held = [pieces[n] for n in HOLD[3]]
    slots = [
        [near, pieces["a1"], two, pieces["a2"], pieces["b"], pieces["c"]],
        [three, pieces["a3"], pieces["b3"], pieces["c3"]],
    ]
    gated = pl.pallas_call(
        waiting(functools.partial(gate_kernel, step), len(held), 12),
        grid=(steps,),
        in_specs=[
            smem,
            wide(rows),
            wide(8),
            taps_spec,
            wide(rows),
            wide(rows),
            wide(subs * modes),
            wide(modes),
            wide(modes),
            wide(modes),
            stack(lag),
            wide(1),
        ]
        + [unused] * len(held),
        out_specs=wide(rows),
        out_shape=jax.ShapeDtypeStruct((rows, chans), bf16),
        compiler_params=params(),
        cost_estimate=COST,
        name="gate",
    )(here, query, halo, taps, kv, inner, before, enter, other, rate_chan, lag, skip[None], *held)
    return gated, slots


def hop(x, first):
    count = lax.axis_size("ctx")
    even, odd = (2, 4) if first else (4, 2)
    return lax.ppermute(x, "ctx", [(i, i ^ (odd if i % 2 else even)) for i in range(count)])


def block_order(index):
    core = index & 1
    block = index & 7
    return [block, block ^ (2 + 2 * core), block ^ (4 - 2 * core), block ^ 6]


def both_rows(mine_ref, other_ref, part, depth):
    at = pl.ds(pl.multiple_of(part * depth, depth), depth)
    return jnp.concatenate([mine_ref[:, at], other_ref[:, at]], axis=0)


def near_kernel(index_ref, place_ref, mine_ref, other_ref, weight_ref, *refs):
    index, place = index_ref[0], place_ref[0]
    near_ref, near_one, two_ref, two_one, side, corner, acc_ref = refs
    depth, block = near_ref.shape
    own, left_one, left_two = [both_rows(mine_ref, other_ref, place ^ n, depth) for n in (0, 1, 2)]
    left = jnp.concatenate([left_one, left_two], axis=1)
    for r, at in enumerate(block_order(index)):
        total = dot(own, weight_ref[:, pl.ds(pl.multiple_of(at * block, block), block)])
        if r < 2:
            one, two = ((near_ref, two_ref), (near_one, two_one))[r]
            total = total + dot(left_one, one[...]) + dot(left_two, two[...])
        else:
            total = total + dot(left, (side, corner)[r - 2][...])
        acc_ref[:, r * block : (r + 1) * block] = total


def far_kernel(first, index_ref, place_ref, gated_ref, *refs):
    index, place = index_ref[0], place_ref[0]
    three, acc_ref, out_ref = refs[:4], refs[4], refs[5]
    depth, block = three[0].shape
    rows = gated_ref.shape[0]
    left = gated_ref[:, pl.ds(pl.multiple_of((place ^ 3) * depth, depth), depth)]
    for r, at in enumerate(block_order(index)):
        total = acc_ref[first : first + rows, r * block : (r + 1) * block] + dot(left, three[r][...])
        cols = pl.ds(pl.multiple_of((at >> 1) * block, block), block)
        out_ref[:, cols] = total.astype(bf16)


def join_kernel(nums_ref, mine_ref, other_ref, out_ref):
    block = mine_ref.shape[1] // 4
    core = nums_ref[0] & 1
    for h in range(4):
        at = pl.multiple_of((2 * h + core) * block, block)
        out_ref[:, pl.ds(at, block)] = mine_ref[:, h * block : (h + 1) * block]
        at = pl.multiple_of((2 * h + 1 - core) * block, block)
        out_ref[:, pl.ds(at, block)] = other_ref[:, h * block : (h + 1) * block]


def project(gated, weight, slots):
    count = lax.axis_size("ctx")
    index = lax.axis_index("ctx")[None].astype(jnp.int32)
    place = lax.axis_index("fsdp")[None].astype(jnp.int32)
    rows = gated.shape[0]
    cols = weight.shape[1]
    swap = [(i, i ^ 1) for i in range(count)]
    other = lax.ppermute(gated, "ctx", swap)
    vmem = pl.BlockSpec(memory_space=pltpu.VMEM)
    smem = pl.BlockSpec(memory_space=pltpu.SMEM)

    def call(kernel, name, shapes, scalars, *args):
        return pl.pallas_call(
            kernel,
            in_specs=[smem] * len(scalars) + [vmem] * len(args),
            out_specs=[vmem] * len(shapes),
            out_shape=shapes,
            compiler_params=params(),
            cost_estimate=COST,
            name=name,
        )(*scalars, *args)

    (acc,) = call(
        near_kernel,
        "project_near",
        [jax.ShapeDtypeStruct((2 * rows, cols // 2), f32)],
        (index, place), gated, other, weight, *slots[0],
    )
    half = [jax.ShapeDtypeStruct((rows, cols // 2), bf16)]
    (theirs,) = call(
        functools.partial(far_kernel, rows), "project_theirs", half, (index, place), other, *slots[1], acc
    )
    back = lax.ppermute(theirs, "ctx", swap)
    (mine,) = call(
        functools.partial(far_kernel, 0), "project_mine", half, (index, place), gated, *slots[1], acc
    )
    (out,) = call(
        join_kernel,
        "join_columns",
        [jax.ShapeDtypeStruct((rows, cols), bf16)],
        (index,), mine, back,
    )
    return out


def local(query_in, key_in, value_in, feature_taps, decay_rate, residues, skip_gain, out_weight):
    query, key, value = query_in[0], key_in[0], value_in[0]
    tails, mine = prepare(query, key, value, out_weight)
    count = lax.axis_size("ctx")
    halo = lax.ppermute(tails, "ctx", [(i, i + 1) for i in range(count - 1)])
    two = lax.ppermute(mine, "fsdp", [(i, i ^ 2) for i in range(4)])
    near = lax.ppermute(mine, "fsdp", [(i, i ^ 1) for i in range(4)])
    gated, slots = conv_path(
        query, key, value, halo, near, two, mine, decay_rate, residues, feature_taps, skip_gain
    )
    return project(gated, out_weight, slots)[None]


def solution(mesh):
    return jax.shard_map(
        local,
        mesh=mesh,
        in_specs=(
            P("fsdp", "ctx", None),
            P("fsdp", "ctx", None),
            P("fsdp", "ctx", None),
            P(),
            P(),
            P(),
            P(),
            P("fsdp", None),
        ),
        out_specs=P("fsdp", "ctx", None),
        check_vma=False,
    )
```

```python
import functools

import jax
import jax.numpy as jnp
from jax import lax
from jax.experimental import pallas as pl
from jax.experimental.pallas import tpu as pltpu
from jax.sharding import PartitionSpec as P

GROUP = 16
HOLD = [[], [], [], []]
RELAY = {'z1': [], 'a1': [], 'mine': ['z1'], 'z2': ['s1'], 'z3': ['s2'], 'a3': []}
FEAT = 3
WIDE = 2048
LANES = 128
SUB = 32
VMEM_LIMIT = 48 << 20
PREP = 61
COST = pl.CostEstimate(flops=0, bytes_accessed=0, transcendentals=0)

bf16 = jnp.bfloat16
f32 = jnp.float32


def waiting(kernel, count, first):
    def body(*refs):
        kernel(*refs[:first], *refs[first + count :])

    return body


def params(limit=VMEM_LIMIT):
    return pltpu.CompilerParams(vmem_limit_bytes=limit)


def split(x):
    high = x.astype(bf16)
    return high, (x - high.astype(f32)).astype(bf16)


def iota(shape, dim):
    return lax.broadcasted_iota(jnp.int32, shape, dim)


def one_less_exp(x):
    small = jnp.minimum(x, 0.5)
    series = jnp.ones_like(x)
    for n in range(9, 1, -1):
        series = 1.0 - small * (1.0 / n) * series
    return jnp.where(x < 0.5, small * series, 1.0 - jnp.exp(-x))


def dot(a, b):
    return jnp.dot(a, b, preferred_element_type=f32)


def featurize(rows, tail, taps):
    values = rows.astype(f32)
    at = iota(values.shape, 0)
    one = jnp.where(at == 0, tail[1:2], pltpu.roll(values, 1, 0))
    two = jnp.where(at == 0, tail[0:1], jnp.where(at == 1, tail[1:2], pltpu.roll(values, 2, 0)))
    return taps[0:1] * values + taps[1:2] * one + taps[2:3] * two


def table_kernel(rate_ref, residue_ref, left_ref, lag_ref, rate_chan_ref):
    rate = rate_ref[...]
    groups, modes = rate.shape
    scale = residue_ref[...] * jnp.sqrt(one_less_exp(2.0 * rate))
    blocks, _, depth = left_ref.shape
    sub = left_ref.shape[1] // 2 - modes
    each = groups // blocks

    def expand(table, width, count):
        pick = iota((groups, count), 0) == iota((groups, count), 1) // width
        pick = pick.astype(bf16)
        high = table.astype(bf16)
        rest = table - high.astype(f32)
        middle, low = split(rest)
        return dot(high, pick) + (dot(middle, pick) + dot(low, pick))

    rate_turned, scale_turned = rate.T, scale.T
    rate_chan_ref[...] = expand(rate_turned, GROUP, groups * GROUP)
    rate_wide = expand(rate_turned, sub, groups * sub)
    scale_wide = expand(scale_turned, sub, groups * sub)
    place = iota((modes, groups * sub), 1) % sub
    back = jnp.where(place == 0, 0, sub - place).astype(f32)
    taps = jnp.sum(scale_wide * jnp.exp(-rate_wide * back), axis=0, keepdims=True)
    ends = scale_wide * jnp.exp(-rate_wide * (sub - 1 - place).astype(f32))
    end_high, end_low = split(ends)
    causal = iota((sub, LANES), 0) >= iota((sub, LANES), 1) % sub
    start = iota((1, LANES), 1) % sub == 0
    spread = rate_chan_ref[...] if modes == GROUP else expand(rate_turned, modes, groups * modes)
    mode_pick = iota((modes, groups * modes), 0) == iota((modes, groups * modes), 1) % modes
    rate_lane = jnp.sum(jnp.where(mode_pick, spread, 0.0), axis=0, keepdims=True)
    ahead = (iota((sub, each * modes), 0) + 1).astype(f32)
    for b in range(blocks):
        for part in range(depth // LANES):
            at = b * depth + part * LANES
            row = taps[:, at : at + LANES]
            row = jnp.where(start, row, pltpu.roll(row, LANES - sub, 1))
            band = pltpu.roll(jnp.broadcast_to(row, (sub, LANES)), 0, 1, stride=1, stride_axis=0)
            high, low = split(jnp.where(causal, band, 0.0))
            to = slice(part * LANES, (part + 1) * LANES)
            left_ref[b, :sub, to] = high
            left_ref[b, sub : 2 * sub, to] = low
        cols = slice(b * depth, (b + 1) * depth)
        left_ref[b, 2 * sub : 2 * sub + modes] = end_high[:, cols]
        left_ref[b, 2 * sub + modes :] = end_low[:, cols]
        lane = rate_lane[:, b * each * modes : (b + 1) * each * modes]
        high, low = split(jnp.exp(-lane * ahead))
        lag_ref[b, :sub] = jnp.concatenate([high, high], axis=1)
        lag_ref[b, sub:] = jnp.concatenate([low, jnp.zeros_like(low)], axis=1)


def own_groups(rows_each):
    rows = LANES // GROUP * rows_each
    return iota((rows, LANES), 0) // rows_each == iota((rows, LANES), 1) // GROUP


def product_kernel(
    key_ref, value_ref, halo_ref, taps_ref, left_ref, rate_ref, kv_ref, inner_ref, before_ref, state_ref
):
    rows, width = key_ref.shape
    modes = rate_ref.shape[0]
    sub = left_ref.shape[1] // 2 - modes
    count = rows // sub
    halo = halo_ref[...]
    key = featurize(key_ref[...], halo[2:4], taps_ref[1])
    value = featurize(value_ref[...], halo[4:6], taps_ref[2])
    kv = (key * value).astype(bf16)
    kv_ref[...] = kv
    same = own_groups(sub)
    fade = jnp.exp(-rate_ref[...] * float(sub))
    for b in range(width // LANES):
        cols = slice(b * LANES, (b + 1) * LANES)
        total = jnp.zeros((modes, LANES), f32)
        for first in range(0, count, 2):
            right = []
            for s in (first, first + 1):
                piece = kv[s * sub : (s + 1) * sub, cols]
                spread = jnp.concatenate([piece] * (LANES // GROUP), axis=0)
                right.append(jnp.where(same, spread, jnp.zeros_like(spread)))
            out = dot(left_ref[b], jnp.concatenate(right, axis=1))
            for s in (first, first + 1):
                part = out[:, (s - first) * LANES : (s - first + 1) * LANES]
                inner_ref[s * sub : (s + 1) * sub, cols] = part[:sub] + part[sub : 2 * sub]
                before_ref[s * modes : (s + 1) * modes, cols] = total
                total = total * fade[:, cols] + (
                    part[2 * sub : 2 * sub + modes] + part[2 * sub + modes :]
                )
        state_ref[:, cols] = total


def blend_kernel(rows, step, where_ref, state_ref, other_ref, enter_ref, rate_ref, new_ref, into_ref):
    index = where_ref[0]
    upper = (index // step) % 2 == 1
    within = ((index % step) * rows).astype(f32)
    rate = rate_ref[...]
    state, other, enter = state_ref[...], other_ref[...], enter_ref[...]
    into_ref[...] = jnp.where(upper, enter + jnp.exp(-rate * within) * other, enter)
    fade = jnp.exp(-rate * float(step * rows))
    new_ref[...] = jnp.where(upper, other * fade + state, state * fade + other)


def gate_kernel(
    step, where_ref, query_ref, halo_ref, taps_ref, kv_ref, inner_ref, before_ref, enter_ref, other_ref,
    rate_ref, lag_ref, skip_ref, out_ref,
):
    rows, width = query_ref.shape
    modes = rate_ref.shape[0]
    sub = lag_ref.shape[1] // 2
    index = where_ref[0]
    upper = (index // step) % 2 == 1
    within = ((index % step) * rows).astype(f32)
    query = featurize(query_ref[...], halo_ref[0:2], taps_ref[0])
    rate = rate_ref[...]
    enter = enter_ref[...]
    enter = jnp.where(upper, enter + jnp.exp(-rate * within) * other_ref[...], enter)
    fade = jnp.exp(-rate * float(sub))
    same = own_groups(modes)
    for b in range(width // LANES):
        cols = slice(b * LANES, (b + 1) * LANES)
        far = enter[:, cols]
        for first in range(0, rows // sub, 2):
            right = []
            for s in (first, first + 1):
                total = far + before_ref[s * modes : (s + 1) * modes, cols]
                spread = jnp.concatenate([total] * (LANES // GROUP), axis=0)
                right.append(jnp.concatenate(split(jnp.where(same, spread, 0.0)), axis=0))
                far = far * fade[:, cols]
            cross = dot(lag_ref[b], jnp.concatenate(right, axis=1))
            for s in (first, first + 1):
                part = cross[:, (s - first) * LANES : (s - first + 1) * LANES]
                at = slice(s * sub, (s + 1) * sub)
                convolved = inner_ref[at, cols] + (part[:sub] + part[sub:])
                convolved = convolved.astype(bf16).astype(f32)
                kv = kv_ref[at, cols].astype(f32)
                out_ref[at, cols] = (query[at, cols] * (convolved + skip_ref[:, cols] * kv)).astype(bf16)


def prepare_kernel(which_ref, query_ref, key_ref, value_ref, weight_ref, tail_ref, piece_ref, rows_ref, sems):
    keep = FEAT - 1
    height = rows_ref.shape[1]
    width = piece_ref.shape[1]
    at = pl.multiple_of((which_ref[0] & 7) * width, width)
    copies = [pltpu.make_async_copy(weight_ref.at[:, pl.ds(at, width)], piece_ref, sems.at[3])]
    for i, ref in enumerate((query_ref, key_ref, value_ref)):
        first = ref.shape[0] - height
        copies.append(
            pltpu.make_async_copy(ref.at[pl.ds(first, height)], rows_ref.at[i], sems.at[i])
        )
    for copy in copies:
        copy.start()
    for copy in copies[1:]:
        copy.wait()
    for i in range(3):
        tail_ref[i * keep : (i + 1) * keep] = rows_ref[i].astype(f32)[height - keep :]
    tail_ref[3 * keep :] = jnp.zeros((tail_ref.shape[0] - 3 * keep, tail_ref.shape[1]), f32)
    copies[0].wait()


def prepare(query, key, value, weight):
    chans = query.shape[1]
    depth, cols = weight.shape
    which = lax.axis_index("ctx")[None].astype(jnp.int32)
    hbm = pl.BlockSpec(memory_space=pltpu.HBM)
    vmem = pl.BlockSpec(memory_space=pltpu.VMEM)
    return pl.pallas_call(
        prepare_kernel,
        in_specs=[pl.BlockSpec(memory_space=pltpu.SMEM)] + [hbm] * 4,
        out_specs=[vmem, vmem],
        out_shape=[
            jax.ShapeDtypeStruct((8, chans), f32),
            jax.ShapeDtypeStruct((depth, cols // 8), bf16),
        ],
        scratch_shapes=[pltpu.VMEM((3, 16, chans), bf16), pltpu.SemaphoreType.DMA((4,))],
        compiler_params=params(PREP << 20),
        name="prepare",
    )(which, query, key, value, weight)


def stack_kernel(one_ref, two_ref, out_ref):
    depth = one_ref.shape[0]
    out_ref[:depth] = one_ref[...]
    out_ref[depth:] = two_ref[...]


def stack_rows(one, two):
    depth, block = one.shape
    vmem = pl.BlockSpec(memory_space=pltpu.VMEM)
    return pl.pallas_call(
        stack_kernel,
        in_specs=[vmem, vmem],
        out_specs=vmem,
        out_shape=jax.ShapeDtypeStruct((2 * depth, block), bf16),
        compiler_params=params(),
        cost_estimate=COST,
        name="stack_rows",
    )(one, two)


def relay_kernel(in_ref, *refs):
    del in_ref, refs


def relay(x, *held):
    unused = pl.BlockSpec(memory_space=pl.ANY)
    return pl.pallas_call(
        relay_kernel,
        in_specs=[unused] * (1 + len(held)),
        out_specs=unused,
        out_shape=jax.ShapeDtypeStruct(x.shape, x.dtype),
        input_output_aliases={0: 0},
        compiler_params=params(),
        cost_estimate=COST,
        name="relay",
    )(x, *held)


def conv_path(query, key, value, halo, near, two, mine, rate, residues, taps, skip):
    rows, chans = query.shape
    groups, modes = rate.shape
    blocks = chans // LANES
    depth = LANES // GROUP * SUB
    count = lax.axis_size("ctx")
    here = lax.axis_index("ctx")[None].astype(jnp.int32)
    steps = chans // WIDE
    per = WIDE // LANES
    vmem = pl.BlockSpec(memory_space=pltpu.VMEM)
    smem = pl.BlockSpec(memory_space=pltpu.SMEM)
    state_shape = jax.ShapeDtypeStruct((modes, chans), f32)
    left, lag, rate_chan = pl.pallas_call(
        table_kernel,
        in_specs=[vmem, vmem],
        out_specs=[vmem] * 3,
        out_shape=[
            jax.ShapeDtypeStruct((blocks, 2 * (SUB + modes), depth), bf16),
            jax.ShapeDtypeStruct((blocks, 2 * SUB, 2 * (LANES // GROUP) * modes), bf16),
            state_shape,
        ],
        compiler_params=params(),
        cost_estimate=COST,
        name="tables",
    )(rate, residues)

    def wide(height):
        return pl.BlockSpec((height, WIDE), lambda b: (0, b))

    def stack(array):
        return pl.BlockSpec((per,) + array.shape[1:], lambda b: (b, 0, 0))

    taps_spec = pl.BlockSpec((3, FEAT, WIDE), lambda b: (0, 0, b))
    subs = rows // SUB
    unused = pl.BlockSpec(memory_space=pl.ANY)
    pieces = dict(z1=near, z2=two)
    held = [pieces[n] for n in HOLD[0]]
    kv, inner, before, state = pl.pallas_call(
        waiting(product_kernel, len(held), 6),
        grid=(steps,),
        in_specs=[wide(rows), wide(rows), wide(8), taps_spec, stack(left), wide(modes)] + [unused] * len(held),
        out_specs=[wide(rows), wide(rows), wide(subs * modes), wide(modes)],
        out_shape=[
            jax.ShapeDtypeStruct((rows, chans), bf16),
            jax.ShapeDtypeStruct((rows, chans), f32),
            jax.ShapeDtypeStruct((subs * modes, chans), f32),
            state_shape,
        ],
        compiler_params=params(),
        cost_estimate=COST,
        name="kv_and_state",
    )(key, value, halo, taps, left, rate_chan, *held)
    enter = jnp.zeros_like(state)
    pieces["k"] = state
    step = 1
    at = lambda array, name: relay(array, *[pieces[n] for n in RELAY[name]]) if RELAY[name] else array
    while True:
        if step == 1:
            near = at(near, "z1")
            pieces["a1"] = hop(near, True)
        other = lax.ppermute(state, "ctx", [(i, i ^ step) for i in range(count)])
        if 2 * step >= count:
            break
        held = [pieces[n] for n in HOLD[1 if step == 1 else 2]]
        state, enter = pl.pallas_call(
            waiting(functools.partial(blend_kernel, rows, step), len(held), 5),
            in_specs=[smem] + [vmem] * 4 + [unused] * len(held),
            out_specs=[vmem] * 2,
            out_shape=[state_shape] * 2,
            compiler_params=params(),
            cost_estimate=COST,
            name="blend_states",
        )(here, state, other, enter, rate_chan, *held)
        if step == 1:
            pieces["s1"] = state
            three = lax.ppermute(at(mine, "mine"), "fsdp", [(i, i ^ 3) for i in range(4)])
            pieces["z3"] = three
        if step == 2:
            pieces["s2"] = state
            two = at(two, "z2")
            pieces["a2"] = hop(two, True)
            pieces["b"] = hop(stack_rows(near, two), False)
            pieces["c"] = hop(stack_rows(pieces["a1"], pieces["a2"]), False)
        step *= 2
    pieces["y"] = other
    three = at(three, "z3")
    pieces["a3"], pieces["b3"] = hop(three, True), hop(three, False)
    pieces["c3"] = hop(at(pieces["a3"], "a3"), False)
    held = [pieces[n] for n in HOLD[3]]
    slots = [
        [near, pieces["a1"], two, pieces["a2"], pieces["b"], pieces["c"]],
        [three, pieces["a3"], pieces["b3"], pieces["c3"]],
    ]
    gated = pl.pallas_call(
        waiting(functools.partial(gate_kernel, step), len(held), 12),
        grid=(steps,),
        in_specs=[
            smem,
            wide(rows),
            wide(8),
            taps_spec,
            wide(rows),
            wide(rows),
            wide(subs * modes),
            wide(modes),
            wide(modes),
            wide(modes),
            stack(lag),
            wide(1),
        ]
        + [unused] * len(held),
        out_specs=wide(rows),
        out_shape=jax.ShapeDtypeStruct((rows, chans), bf16),
        compiler_params=params(),
        cost_estimate=COST,
        name="gate",
    )(here, query, halo, taps, kv, inner, before, enter, other, rate_chan, lag, skip[None], *held)
    return gated, slots


def hop(x, first):
    count = lax.axis_size("ctx")
    even, odd = (2, 4) if first else (4, 2)
    return lax.ppermute(x, "ctx", [(i, i ^ (odd if i % 2 else even)) for i in range(count)])


def block_order(index):
    core = index & 1
    block = index & 7
    return [block, block ^ (2 + 2 * core), block ^ (4 - 2 * core), block ^ 6]


def both_rows(mine_ref, other_ref, part, depth):
    at = pl.ds(pl.multiple_of(part * depth, depth), depth)
    return jnp.concatenate([mine_ref[:, at], other_ref[:, at]], axis=0)


def near_kernel(index_ref, place_ref, mine_ref, other_ref, weight_ref, *refs):
    index, place = index_ref[0], place_ref[0]
    near_ref, near_one, two_ref, two_one, side, corner, acc_ref = refs
    depth, block = near_ref.shape
    own, left_one, left_two = [both_rows(mine_ref, other_ref, place ^ n, depth) for n in (0, 1, 2)]
    left = jnp.concatenate([left_one, left_two], axis=1)
    for r, at in enumerate(block_order(index)):
        total = dot(own, weight_ref[:, pl.ds(pl.multiple_of(at * block, block), block)])
        if r < 2:
            one, two = ((near_ref, two_ref), (near_one, two_one))[r]
            total = total + dot(left_one, one[...]) + dot(left_two, two[...])
        else:
            total = total + dot(left, (side, corner)[r - 2][...])
        acc_ref[:, r * block : (r + 1) * block] = total


def far_kernel(first, index_ref, place_ref, gated_ref, *refs):
    index, place = index_ref[0], place_ref[0]
    three, acc_ref, out_ref = refs[:4], refs[4], refs[5]
    depth, block = three[0].shape
    rows = gated_ref.shape[0]
    left = gated_ref[:, pl.ds(pl.multiple_of((place ^ 3) * depth, depth), depth)]
    for r, at in enumerate(block_order(index)):
        total = acc_ref[first : first + rows, r * block : (r + 1) * block] + dot(left, three[r][...])
        cols = pl.ds(pl.multiple_of((at >> 1) * block, block), block)
        out_ref[:, cols] = total.astype(bf16)


def join_kernel(nums_ref, mine_ref, other_ref, out_ref):
    block = mine_ref.shape[1] // 4
    core = nums_ref[0] & 1
    for h in range(4):
        at = pl.multiple_of((2 * h + core) * block, block)
        out_ref[:, pl.ds(at, block)] = mine_ref[:, h * block : (h + 1) * block]
        at = pl.multiple_of((2 * h + 1 - core) * block, block)
        out_ref[:, pl.ds(at, block)] = other_ref[:, h * block : (h + 1) * block]


def project(gated, weight, slots):
    count = lax.axis_size("ctx")
    index = lax.axis_index("ctx")[None].astype(jnp.int32)
    place = lax.axis_index("fsdp")[None].astype(jnp.int32)
    rows = gated.shape[0]
    cols = weight.shape[1]
    swap = [(i, i ^ 1) for i in range(count)]
    other = lax.ppermute(gated, "ctx", swap)
    vmem = pl.BlockSpec(memory_space=pltpu.VMEM)
    smem = pl.BlockSpec(memory_space=pltpu.SMEM)

    def call(kernel, name, shapes, scalars, *args):
        return pl.pallas_call(
            kernel,
            in_specs=[smem] * len(scalars) + [vmem] * len(args),
            out_specs=[vmem] * len(shapes),
            out_shape=shapes,
            compiler_params=params(),
            cost_estimate=COST,
            name=name,
        )(*scalars, *args)

    (acc,) = call(
        near_kernel,
        "project_near",
        [jax.ShapeDtypeStruct((2 * rows, cols // 2), f32)],
        (index, place), gated, other, weight, *slots[0],
    )
    half = [jax.ShapeDtypeStruct((rows, cols // 2), bf16)]
    (theirs,) = call(
        functools.partial(far_kernel, rows), "project_theirs", half, (index, place), other, *slots[1], acc
    )
    back = lax.ppermute(theirs, "ctx", swap)
    (mine,) = call(
        functools.partial(far_kernel, 0), "project_mine", half, (index, place), gated, *slots[1], acc
    )
    (out,) = call(
        join_kernel,
        "join_columns",
        [jax.ShapeDtypeStruct((rows, cols), bf16)],
        (index,), mine, back,
    )
    return out


def local(query_in, key_in, value_in, feature_taps, decay_rate, residues, skip_gain, out_weight):
    query, key, value = query_in[0], key_in[0], value_in[0]
    tails, mine = prepare(query, key, value, out_weight)
    count = lax.axis_size("ctx")
    halo = lax.ppermute(tails, "ctx", [(i, i + 1) for i in range(count - 1)])
    two = lax.ppermute(mine, "fsdp", [(i, i ^ 2) for i in range(4)])
    near = lax.ppermute(mine, "fsdp", [(i, i ^ 1) for i in range(4)])
    gated, slots = conv_path(
        query, key, value, halo, near, two, mine, decay_rate, residues, feature_taps, skip_gain
    )
    return project(gated, out_weight, slots)[None]


def solution(mesh):
    return jax.shard_map(
        local,
        mesh=mesh,
        in_specs=(
            P("fsdp", "ctx", None),
            P("fsdp", "ctx", None),
            P("fsdp", "ctx", None),
            P(),
            P(),
            P(),
            P(),
            P("fsdp", None),
        ),
        out_specs=P("fsdp", "ctx", None),
        check_vma=False,
    )
```
